128 devices in a mesh: row: 16 (over x, z), col: 8 (over y, core).
Axes of the slice: x: 4, y: 4, z: 4, core: 2. Of those that a mesh axis runs over, the one named last changes fastest.
Arguments:
- parent_front: float32 [128, 128, 128, 128], P('row', 'col'), as said below
- child_updates: float32 [128, 64, 128, 128], P('row', 'col'), as said below
- child_mask: int32 [128, 64], P('row', 'col'), may hold values from 0 to 1, as said below
- child_map: int32 [2, 64], replicated, may hold values from 0 to 127, as said below
Outputs:
- factored: float32 [128, 128, 128, 128], P('row', 'col')
The draws below stay inside these ranges and needn't reach their ends.
Inputs may be any that keep to these rules, and one draw needn't show every extreme that they name: `parent_front`: symmetric as a matrix of order 16384; with any admissible child updates the assembled front is positive definite. `child_updates`: each child's update is symmetric as a matrix of order 64 * 128. `child_mask`: symmetric for each child: block (a, b) is nonzero exactly when block (b, a) is. `child_map`: the 64 entries of one child are distinct. For each child and each t < 8, among the child blocks t + 8 i at most 1 share a residue modulo 2 * 8 and at most 1 share a residue modulo 8; both bounds are reached in every draw.
All inputs are finite; a program needn't handle non-finite values.
Results may differ from the reference program's by a relative error of at most 0.00005.
Values sent between devices are 32-bit elements; how exact they have to be, the bound alone decides.
No kernel may reach another device: no remote copies, remote signals or barrier semaphores. Data moves between devices by JAX's collectives and lax.ppermute only.
A program may use at most 128 MiB of HBM per device.

```python
import math
import jax
import jax.numpy as jnp
from jax import lax

B = 128
LR = 8
CBD = 8
PW = 4
PANELS = 2
NB = 128
LC = 16
F = 16384
CG = 8
NCB = 64
N_ROW = 16
N_COL = 8


def draw_parent_front(key, part):
    key = jax.random.fold_in(key, 21)
    noise_key, height_key = jax.random.split(key)
    noise = jax.random.normal(noise_key, (NB, NB, B, B), jnp.float32)
    symmetric = (noise + noise.transpose(1, 0, 3, 2)) * 0.7071
    base_height = 1.2 * (2.0 * math.sqrt(F) + 4.0 * math.sqrt(NCB * B))
    heights = base_height * jax.random.uniform(height_key, (NB, B), jnp.float32, 1.0, 2.0)
    same_block = (jnp.arange(NB)[:, None] == jnp.arange(NB)[None, :]).astype(jnp.float32)
    same_entry = jnp.eye(B, dtype=jnp.float32)
    diagonal = same_block[:, :, None, None] * same_entry[None, None] * heights[:, None, :, None]
    row_place = jnp.arange(NB)[:, None, None, None] * B + jnp.arange(B)[None, None, :, None]
    col_place = jnp.arange(NB)[None, :, None, None] * B + jnp.arange(B)[None, None, None, :]
    distance = jnp.abs(row_place - col_place).astype(jnp.float32)
    coupling = 16.0 * jnp.exp(-distance * (4.0 / F))
    full_front = symmetric + diagonal + coupling
    grid = full_front.reshape(LR, NB // LR, LC, NB // LC, B, B).transpose(1, 0, 3, 2, 4, 5)
    return grid.reshape(NB, NB, B, B)


def draw_child_updates(key, part):
    key = jax.random.fold_in(key, 22)
    noise = jax.random.normal(key, (2, NCB, NCB, B, B), jnp.float32)
    symmetric = (noise + noise.transpose(0, 2, 1, 4, 3)) * 0.7071
    grid = symmetric.reshape(2, CBD, CG, CBD, CG, B, B).transpose(0, 2, 1, 4, 3, 5, 6)
    return grid.reshape(2 * NCB, NCB, B, B)


def draw_child_mask(key, part):
    key = jax.random.fold_in(key, 23)
    raw_bits = (jax.random.randint(key, (2, NCB, NCB), 0, 10) > 0).astype(jnp.int32)
    both_ways = raw_bits * raw_bits.transpose(0, 2, 1)
    grid = both_ways.reshape(2, CBD, CG, CBD, CG).transpose(0, 2, 1, 4, 3)
    return grid.reshape(2 * NCB, NCB).astype(jnp.int32)


def draw_child_map(key, part):
    key = jax.random.fold_in(key, 24)
    keys = jax.random.split(key, 4)
    order_keys = jax.random.split(keys[0], 2 * CG)
    orders = jax.vmap(lambda subkey: jax.random.permutation(subkey, CG))(order_keys).reshape(2, CG, CG)
    flips = jax.random.randint(keys[1], (2, CG, CG), 0, 2)
    band_keys = jax.random.split(keys[2], 2)
    bands = jax.vmap(lambda subkey: jax.random.permutation(subkey, LR)[:CG])(band_keys)
    shifts = jax.random.randint(keys[3], (2, 2 * CG), 0, LR)
    inside = jnp.arange(CBD)
    lowpart = inside % CG
    highpart = inside // CG
    residue = orders[:, :, lowpart] + CG * ((highpart[None, None, :] + flips[:, :, lowpart]) % 2)
    moved = jnp.take_along_axis(shifts, residue.reshape(2, CG * CBD), axis=1).reshape(2, CG, CBD)
    upper_index = (bands[:, :, None] + moved) % LR
    targets = upper_index * (2 * CG) + residue
    return targets.transpose(0, 2, 1).reshape(2, NCB).astype(jnp.int32)


def setup_inputs(seed: int = 0) -> dict:
    key_list = jax.random.split(jax.random.key(seed), 5)
    parent_front = draw_parent_front(jax.random.fold_in(key_list[4], 71), 0)
    child_updates = draw_child_updates(jax.random.fold_in(key_list[4], 71), 0)
    child_mask = draw_child_mask(jax.random.fold_in(key_list[4], 71), 0)
    child_map = draw_child_map(jax.random.fold_in(key_list[4], 71), 0)
    return {"parent_front": parent_front, "child_updates": child_updates, "child_mask": child_mask, "child_map": child_map}


def stored_to_global(stored):
    grid = stored.reshape(N_ROW, LR, N_COL, LC, B, B).transpose(1, 0, 3, 2, 4, 5)
    return grid.reshape(NB, NB, B, B)

def matrix_to_stored(matrix):
    grid = matrix.reshape(NB, B, NB, B).transpose(0, 2, 1, 3).reshape(LR, N_ROW, LC, N_COL, B, B)
    return grid.transpose(1, 0, 3, 2, 4, 5).reshape(NB, NB, B, B)

def reference(parent_front, child_updates, child_mask, child_map):
    blocks = stored_to_global(parent_front)
    updates = child_updates.reshape(2, N_COL, CBD, N_COL, CBD, B, B).transpose(0, 2, 1, 4, 3, 5, 6)
    updates = updates.reshape(2, NCB, NCB, B, B)
    weights = child_mask.reshape(2, N_COL, CBD, N_COL, CBD).transpose(0, 2, 1, 4, 3)
    weights = weights.reshape(2, NCB, NCB).astype(jnp.float32)
    for child_index in range(2):
        targets = child_map[child_index]
        blocks = blocks.at[targets[:, None], targets[None, :]].add(updates[child_index] * weights[child_index][:, :, None, None])
    matrix = blocks.transpose(0, 2, 1, 3).reshape(F, F)
    leading = PANELS * PW * B
    factor = jnp.linalg.cholesky(matrix[:leading, :leading])
    below_part = lax.linalg.triangular_solve(factor, matrix[leading:, :leading].T, left_side=True, lower=True).T
    schur = matrix[leading:, leading:] - jnp.dot(below_part, below_part.T, precision=lax.Precision.HIGHEST)
    column_part = jnp.concatenate([factor, below_part], axis=0)
    other_part = jnp.concatenate([matrix[:leading, leading:], schur], axis=0)
    return matrix_to_stored(jnp.concatenate([column_part, other_part], axis=1))
```

```python
import jax
import jax.numpy as jnp
from jax import lax
from jax.experimental import pallas as pl
from jax.experimental.pallas import tpu as pltpu
from jax.sharding import PartitionSpec as P

B = 128
HB = 64
ROWS = 16
COLS = 8
HALF = 8
LR = 8
LC = 16
CB = 8
PANEL = 1024
f32 = jnp.float32
bf16 = jnp.bfloat16
exact = lax.Precision.HIGHEST
MIB = 2**20


def block_dot(left, right, contract_left=1):
    dims = (((contract_left,), (0,)), ((), ()))
    return lax.dot_general(left, right, dims, preferred_element_type=f32)


def exact_dot(left, right, contract_left=1):
    dims = (((contract_left,), (0,)), ((), ()))
    return lax.dot_general(left, right, dims, precision=exact, preferred_element_type=f32)


def split(value):
    high = value.astype(bf16)
    return high, (value - high.astype(f32)).astype(bf16)


def slot_first(match, dup):
    return jnp.maximum(jnp.where(match > 0, match, dup) - 1, 0)


def pack_slots(child, table, second):
    def pick(step, tab):
        match = tab[step]
        if second:
            return jnp.maximum(match - 1, 0), 0, 1, 0, 0
        dup = tab[ROWS + step]
        lower = jnp.logical_and(match == 0, dup > 0).astype(jnp.int32)
        return slot_first(match, dup), 0, lower, 0, 0

    def body(tab, child_ref, out_ref):
        step = pl.program_id(0)
        match = tab[step]
        dup = tab[ROWS + step]
        if second:
            used = match > 0
            row = jnp.maximum(match - 1, 0)
        else:
            used = jnp.logical_or(match > 0, dup > 0)
            row = slot_first(match, dup)
        for place in range(COLS):
            source = tab[2 * ROWS + place]
            kept = tab[2 * ROWS + COLS + row * CB + source]
            gain = jnp.where(used, kept, 0).astype(f32)
            out_ref[0, place] = child_ref[0, source, 0] * gain

    return pl.pallas_call(
        body,
        grid_spec=pltpu.PrefetchScalarGridSpec(
            num_scalar_prefetch=1,
            grid=(ROWS,),
            in_specs=[pl.BlockSpec((1, CB, 1, HB, B), pick)],
            out_specs=pl.BlockSpec((1, COLS, HB, B), lambda step, tab: (step, 0, 0, 0)),
        ),
        out_shape=jax.ShapeDtypeStruct((ROWS, COLS, HB, B), f32),
        compiler_params=pltpu.CompilerParams(vmem_limit_bytes=16 * MIB),
        cost_estimate=pl.CostEstimate(flops=2**20, bytes_accessed=8 * MIB, transcendentals=0),
    )(table, child)


def gain_of(code):
    return (code > 0).astype(f32)


def place_of(code):
    return jnp.maximum(code - 1, 0)


NKEYS = LR + 1 + LC


def leading_row(front, received, arrived, table):
    def body(tab, own_ref, recv_ref, first_ref, other_ref, top_ref, even_ref, odd_ref, lead_ref):
        upper = tab[2 * NKEYS] < HALF
        side = tab[2 * NKEYS] // HALF
        for m in range(LC):
            value = jnp.where(upper, own_ref[0, m, 0], recv_ref[m])
            for child, ref in ((0, first_ref), (1, other_ref)):
                base = child * NKEYS
                code = tab[base + LR + 1 + m]
                gain = gain_of(code) * gain_of(tab[base + LR])
                value = value + ref[0, place_of(code)] * gain
            top_ref[m] = value
        lead_ref[...] = top_ref[0]
        for l in range(LR):
            even_ref[l] = top_ref[2 * l + side]
            odd_ref[l] = top_ref[2 * l + 1 - side]

    def rows_of(child):
        return lambda step, tab: (child * HALF + place_of(tab[child * NKEYS + LR]), 0, 0, 0)

    return pl.pallas_call(
        body,
        grid_spec=pltpu.PrefetchScalarGridSpec(
            num_scalar_prefetch=1,
            grid=(1,),
            in_specs=[
                pl.BlockSpec((1, LC, 1, HB, B), lambda step, tab: (0, 0, 0, 0, 0)),
                pl.BlockSpec((LC, HB, B), lambda step, tab: (0, 0, 0)),
                pl.BlockSpec((1, COLS, HB, B), rows_of(0)),
                pl.BlockSpec((1, COLS, HB, B), rows_of(1)),
            ],
            out_specs=[
                pl.BlockSpec((LC, HB, B), lambda step, tab: (0, 0, 0)),
                pl.BlockSpec((LR, HB, B), lambda step, tab: (0, 0, 0)),
                pl.BlockSpec((LR, HB, B), lambda step, tab: (0, 0, 0)),
                pl.BlockSpec((HB, B), lambda step, tab: (0, 0)),
            ],
        ),
        out_shape=[
            jax.ShapeDtypeStruct((LC, HB, B), f32),
            jax.ShapeDtypeStruct((LR, HB, B), f32),
            jax.ShapeDtypeStruct((LR, HB, B), f32),
            jax.ShapeDtypeStruct((HB, B), f32),
        ],
        compiler_params=pltpu.CompilerParams(vmem_limit_bytes=16 * MIB),
        cost_estimate=pl.CostEstimate(flops=2**20, bytes_accessed=3 * MIB, transcendentals=0),
    )(table, front, received, arrived, arrived)


def extend_add(front, arrived, table, half):
    def body(tab, parent_ref, first_ref, other_ref, out_ref):
        step = pl.program_id(0)
        for m in range(LC):
            value = parent_ref[0, m, 0]
            for child, ref in ((0, first_ref), (1, other_ref)):
                base = child * NKEYS
                code = tab[base + LR + 1 + m]
                gain = gain_of(code) * gain_of(tab[base + step])
                value = value + ref[0, place_of(code)] * gain
            out_ref[0, m] = value

    def rows_of(child):
        return lambda step, tab: (child * HALF + place_of(tab[child * NKEYS + step]), 0, 0, 0)

    return pl.pallas_call(
        body,
        grid_spec=pltpu.PrefetchScalarGridSpec(
            num_scalar_prefetch=1,
            grid=(LR,),
            in_specs=[
                pl.BlockSpec((1, LC, 1, HB, B), lambda step, tab: (step, 0, half, 0, 0)),
                pl.BlockSpec((1, COLS, HB, B), rows_of(0)),
                pl.BlockSpec((1, COLS, HB, B), rows_of(1)),
            ],
            out_specs=pl.BlockSpec((1, LC, HB, B), lambda step, tab: (step, 0, 0, 0)),
        ),
        out_shape=jax.ShapeDtypeStruct((LR, LC, HB, B), f32),
        compiler_params=pltpu.CompilerParams(vmem_limit_bytes=16 * MIB),
        cost_estimate=pl.CostEstimate(flops=2**21, bytes_accessed=12 * MIB, transcendentals=0),
    )(table, front, arrived, arrived)


def factor_block(block):
    lane = lax.broadcasted_iota(jnp.int32, (8, B), 1)
    sub = lax.broadcasted_iota(jnp.int32, (8, B), 0)

    def lanes(tile, j):
        return jnp.broadcast_to(tile[:, j : j + 1], (8, B))

    def subs(tile, k):
        return jnp.broadcast_to(tile[k : k + 1, :], (8, B))

    tiles = [block[8 * r : 8 * r + 8, :] for r in range(B // 8)]
    for group in range(B // 8):
        low = 8 * group
        rest = range(group + 1, B // 8)
        own = [lanes(tiles[group], low + k) for k in range(8)]
        far = {r: [lanes(tiles[r], low + k) for k in range(8)] for r in rest}
        inside = jnp.logical_and(lane >= low, lane < low + 8)
        scaled = []
        for k in range(8):
            inv = 1.0 / subs(own[k], k)
            here = lane == low + k
            row = jnp.where(here, 1.0, subs(tiles[group], k)) * inv
            later = jnp.logical_and(lane > low + k, lane < low + 8)
            scaled.append(jnp.where(later, 0.0, row))
            steps = {m: subs(own[m], k) * inv for m in range(k + 1, 8)}
            if k < 7:
                below = sub > k
                coef = jnp.where(below, own[k], 0.0)
                clear = jnp.logical_and(below, here)
                tiles[group] = jnp.where(clear, 0.0, tiles[group]) - coef * row
                for m in range(k + 1, 8):
                    own[m] = own[m] - coef * steps[m]
            for r in rest:
                for m in range(k + 1, 8):
                    far[r][m] = far[r][m] - far[r][k] * steps[m]
        for r in rest:
            value = jnp.where(inside, 0.0, tiles[r])
            for k in range(8):
                value = value - far[r][k] * scaled[k]
            tiles[r] = value
    return jnp.concatenate(tiles, axis=0)


def leading_factor(pieces, where):
    def body(at, *refs):
        piece_refs, (w, diag) = refs[:8], refs[8:]
        for n, ref in enumerate(piece_refs):
            dk, dy = n // 4, n % 4
            q = ((at[2] + dy) % 4) * 2 + (at[3] + dk) % 2
            for dx in range(4):
                x = (at[0] + dx) % 4
                for dz in range(4):
                    g = (x % 2) * 4 + (at[1] + dz) % 4
                    top = pl.multiple_of(g * B + (x // 2) * HB, HB)
                    w[pl.ds(top, HB), pl.ds(pl.multiple_of(q * B, B), B)] = ref[dx, dz]
        row = lax.broadcasted_iota(jnp.int32, (B, B), 0)
        col = lax.broadcasted_iota(jnp.int32, (B, B), 1)

        def step(kb, carry):
            o = pl.multiple_of(kb * B, B)
            f = factor_block(w[pl.ds(o, B), pl.ds(o, B)])
            pivots = jnp.sum(jnp.where(row == col, f, 0.0), axis=1, keepdims=True)
            scale = 1.0 / jnp.sqrt(pivots)
            inverse = jnp.where(row > col, f, (row == col).astype(f32)) * scale
            diag[pl.ds(o, B), :] = jnp.where(row <= col, f, 0.0) * scale
            w[pl.ds(o, B), :] = exact_dot(inverse, w[pl.ds(o, B), :])
            w[pl.ds(o, B), pl.ds(o, B)] = inverse

            @pl.when(kb % 2 == 0)
            def _():
                n = pl.multiple_of(o + B, B)
                w[pl.ds(n, B), pl.ds(o, B)] = jnp.zeros((B, B), f32)
                w[pl.ds(n, B), :] -= exact_dot(w[pl.ds(o, B), pl.ds(n, B)], w[pl.ds(o, B), :], 0)

            for done in range(256, PANEL, 256):

                @pl.when(kb == done // B - 1)
                def _():
                    above = (slice(done - 256, done - B), slice(done - B, done))
                    kept = w[above]
                    w[above] = jnp.zeros((B, B), f32)
                    w[done:, done - 256 : done] = jnp.zeros((PANEL - done, 256), f32)
                    for n in range(done, PANEL, 256):
                        left = w[done - 256 : done, n : n + 256]
                        w[n : n + 256, :] -= exact_dot(left, w[done - 256 : done, :], 0)
                    w[above] = kept

            return carry

        lax.fori_loop(0, PANEL // B, step, 0)

    return pl.pallas_call(
        body,
        in_specs=[pl.BlockSpec(memory_space=pltpu.SMEM)]
        + [pl.BlockSpec(memory_space=pltpu.VMEM)] * 8,
        out_specs=[pl.BlockSpec(memory_space=pltpu.VMEM)] * 2,
        out_shape=[
            jax.ShapeDtypeStruct((PANEL, PANEL), f32),
            jax.ShapeDtypeStruct((PANEL, B), f32),
        ],
        compiler_params=pltpu.CompilerParams(vmem_limit_bytes=40 * MIB),
        cost_estimate=pl.CostEstimate(
            flops=50 * 2**30, bytes_accessed=9 * MIB, transcendentals=1024
        ),
    )(where, *pieces)


def panel_solve(rows, w, diag, where):
    def body(at, rows_ref, w_ref, diag_ref, high_ref, low_ref, out_ref, gh, gl, wh, wl, bt, bh, bl):
        p, q = at[0], at[1]
        side = p // HALF
        for e in range(COLS):
            for order in range(2):
                half = side if order == 0 else 1 - side
                top = pl.multiple_of(e * B + half * HB, HB)
                for l in range(LR):
                    high, low = split(rows_ref[e, order, l])
                    gh[pl.ds(top, HB), l * B : (l + 1) * B] = high
                    gl[pl.ds(top, HB), l * B : (l + 1) * B] = low
        for r in range(0, PANEL, 256):
            shape = (256, r + 256)
            under = (
                lax.broadcasted_iota(jnp.int32, shape, 0) + r
                >= lax.broadcasted_iota(jnp.int32, shape, 1)
            )
            high, low = split(jnp.where(under, w_ref[r : r + 256, : r + 256], 0.0))
            wh[r : r + 256, : r + 256] = high
            wl[r : r + 256, : r + 256] = low
            value = block_dot(high, gh[: r + 256, :])
            value += block_dot(high, gl[: r + 256, :])
            value += block_dot(low, gh[: r + 256, :])
            bt[r : r + 256, :] = value
            high, low = split(value)
            bh[r : r + 256, :] = high
            bl[r : r + 256, :] = low
        mine = pl.ds(pl.multiple_of(q * B, B), B)
        for l in range(LR):
            out_ref[l] = bt[mine, l * B : (l + 1) * B].T

        @pl.when(p < HALF)
        def _():
            over = w_ref[mine, pl.ds(pl.multiple_of((p % HALF) * B, B), B)]
            top = jnp.where(p > q, over, jnp.where(p == q, diag_ref[mine, :], 0.0))
            out_ref[0] = top.T

        for r in range(0, PANEL, 256):
            value = block_dot(wh[r:, r : r + 256], bh[r:, :], 0)
            value += block_dot(wh[r:, r : r + 256], bl[r:, :], 0)
            value += block_dot(wl[r:, r : r + 256], bh[r:, :], 0)
            for l in range(LR):
                for n in range(0, 256, B):
                    high, low = split(value[n : n + B, l * B : (l + 1) * B].T)
                    high_ref[l * B : (l + 1) * B, r + n : r + n + B] = high
                    low_ref[l * B : (l + 1) * B, r + n : r + n + B] = low

        @pl.when(p < HALF)
        def _():
            high_ref[:B, :] = jnp.zeros((B, PANEL), bf16)
            low_ref[:B, :] = jnp.zeros((B, PANEL), bf16)

    return pl.pallas_call(
        body,
        in_specs=[pl.BlockSpec(memory_space=pltpu.SMEM)]
        + [pl.BlockSpec(memory_space=pltpu.VMEM)] * 3,
        out_specs=[pl.BlockSpec(memory_space=pltpu.VMEM)] * 3,
        out_shape=[
            jax.ShapeDtypeStruct((PANEL, PANEL), bf16),
            jax.ShapeDtypeStruct((PANEL, PANEL), bf16),
            jax.ShapeDtypeStruct((LR, B, B), f32),
        ],
        scratch_shapes=[
            pltpu.VMEM((PANEL, PANEL), bf16),
            pltpu.VMEM((PANEL, PANEL), bf16),
            pltpu.VMEM((PANEL, PANEL), bf16),
            pltpu.VMEM((PANEL, PANEL), bf16),
            pltpu.VMEM((PANEL, PANEL), f32),
            pltpu.VMEM((PANEL, PANEL), bf16),
            pltpu.VMEM((PANEL, PANEL), bf16),
        ],
        compiler_params=pltpu.CompilerParams(vmem_limit_bytes=48 * MIB),
        cost_estimate=pl.CostEstimate(
            flops=8 * 2**30, bytes_accessed=14 * MIB, transcendentals=0
        ),
    )(where, rows, w, diag)


def trailing_update(upper, lower, columns, high, low, panel):
    def body(upper_ref, lower_ref, col_ref, high_ref, low_ref, panel_ref, out_ref, ch, cl):
        for p in range(ROWS):
            top = (p % HALF) * B + (p // HALF) * HB
            for n in range(2):
                hi, lo = split(col_ref[p, n])
                ch[top : top + HB, n * B : (n + 1) * B] = hi
                cl[top : top + HB, n * B : (n + 1) * B] = lo
        for r in range(0, PANEL, 256):
            value = block_dot(high_ref[r : r + 256, :], ch[...])
            value += block_dot(high_ref[r : r + 256, :], cl[...])
            value += block_dot(low_ref[r : r + 256, :], ch[...])
            for l in range(r // B, r // B + 2):
                for n in range(2):
                    s = l * B - r
                    cols = slice(n * B, (n + 1) * B)
                    out_ref[l, n, :HB] = upper_ref[l, n] - value[s : s + HB, cols]
                    out_ref[l, n, HB:] = lower_ref[l, n] - value[s + HB : s + B, cols]

        @pl.when(pl.program_id(0) == 0)
        def _():
            for l in range(LR):
                out_ref[l, 0] = panel_ref[l]

    half = pl.BlockSpec((LR, 2, HB, B), lambda step: (0, step, 0, 0))
    whole = pl.BlockSpec((PANEL, PANEL), lambda step: (0, 0))
    return pl.pallas_call(
        body,
        grid=(LC // 2,),
        in_specs=[
            half,
            half,
            pl.BlockSpec((ROWS, 2, HB, B), lambda step: (0, step, 0, 0)),
            whole,
            whole,
            pl.BlockSpec((LR, B, B), lambda step: (0, 0, 0)),
        ],
        out_specs=pl.BlockSpec((LR, 2, B, B), lambda step: (0, step, 0, 0)),
        out_shape=jax.ShapeDtypeStruct((LR, LC, B, B), f32),
        scratch_shapes=[pltpu.VMEM((PANEL, 256), bf16), pltpu.VMEM((PANEL, 256), bf16)],
        compiler_params=pltpu.CompilerParams(vmem_limit_bytes=40 * MIB),
        cost_estimate=pl.CostEstimate(
            flops=12 * 2**30, bytes_accessed=28 * MIB, transcendentals=0
        ),
    )(upper, lower, columns, high, low, panel)


def along_x(distance):
    return [(4 * ((x + distance) % 4) + z, 4 * x + z) for x in range(4) for z in range(4)]


def along_z(distance):
    return [(4 * x + (z + distance) % 4, 4 * x + z) for x in range(4) for z in range(4)]


def along_y(distance):
    return [(2 * ((y + distance) % 4) + k, 2 * y + k) for y in range(4) for k in range(2)]


OTHER_CORE = [(q, q ^ 1) for q in range(COLS)]


def transposed(same):
    pairs = []
    for p in range(ROWS):
        for q in range(COLS):
            side = p // HALF if same else 1 - p // HALF
            pairs.append((p * COLS + q, (q + HALF * side) * COLS + p % HALF))
    return pairs


def shards(parent_front, child_updates, child_mask, child_map):
    p = lax.axis_index("row")
    q = lax.axis_index("col")
    both = ("row", "col")
    front = parent_front.reshape(LR, LC, 2, HB, B)
    child = child_updates.reshape(CB, CB, 2, HB, B)

    own_map = child_map[p // HALF].reshape(CB, CB)
    row_parent = own_map[:, p % HALF]
    col_parent = own_map[:, q]
    index = jnp.arange(CB)
    slots = jnp.arange(ROWS)
    match = jnp.sum((row_parent[None] % ROWS == slots[:, None]) * (index + 1)[None], axis=1)
    dup = jnp.sum((row_parent[None] + HALF == slots[:, None]) * (index + 1)[None], axis=1)
    column = jnp.sum((col_parent[None] % COLS == index[:, None]) * index[None], axis=1)
    source_table = jnp.concatenate([match, dup, column, child_mask.reshape(-1)]).astype(jnp.int32)

    keys = jnp.concatenate(
        [jnp.arange(LR) * ROWS + p, (p % HALF)[None], jnp.arange(LC) * COLS + q]
    )
    hits = child_map[:, None, :] == keys[None, :, None]
    codes = jnp.sum(hits * (jnp.arange(CB * CB) % CB + 1)[None, None], axis=2)
    target_table = jnp.concatenate([codes.reshape(-1), p[None]]).astype(jnp.int32)

    top_other = lax.ppermute(front[0, :, 1], "row", [(i, i + HALF) for i in range(HALF)])

    first = pack_slots(child, source_table, False)
    first = lax.all_to_all(
        first.reshape(ROWS * COLS, HB, B), both, 0, 0, tiled=True
    ).reshape(ROWS, COLS, HB, B)
    second = pack_slots(child, source_table, True)

    top, even, odd, lead = leading_row(front, top_other, first, target_table)

    near = [lead] + [lax.ppermute(lead, "row", along_z(d)) for d in range(1, 4)]
    stacked = jnp.stack(near)
    near = [stacked] + [lax.ppermute(stacked, "row", along_x(d)) for d in range(1, 4)]
    stacked = jnp.stack(near)
    near = [stacked] + [lax.ppermute(stacked, "col", along_y(d)) for d in range(1, 4)]
    near = near + [lax.ppermute(piece, "col", OTHER_CORE) for piece in near]

    turned = jnp.stack(
        [lax.ppermute(even, both, transposed(True)), lax.ppermute(odd, both, transposed(False))]
    )
    panel_rows = lax.all_gather(turned, "col", axis=0)
    columns = lax.all_gather(top, "row", axis=0)

    second = lax.all_to_all(
        second.reshape(ROWS * COLS, HB, B), both, 0, 0, tiled=True
    ).reshape(ROWS, COLS, HB, B)
    upper = extend_add(front, first, target_table, 0)

    where = jnp.stack([p // 4, p % 4, q // 2, q % 2]).astype(jnp.int32)
    w, diag = leading_factor(near, where)
    high, low, panel = panel_solve(panel_rows, w, diag, jnp.stack([p, q]).astype(jnp.int32))
    lower = extend_add(front, second, target_table, 1)
    return trailing_update(upper, lower, columns, high, low, panel)


def solution(mesh):
    in_specs = (P("row", "col", None, None), P("row", "col", None, None), P("row", "col"), P())
    out_specs = P("row", "col", None, None)
    return jax.shard_map(shards, mesh=mesh, in_specs=in_specs, out_specs=out_specs, check_vma=False)
```

```python
import jax
import jax.numpy as jnp
from jax import lax
from jax.experimental import pallas as pl
from jax.experimental.pallas import tpu as pltpu
from jax.sharding import PartitionSpec as P

B = 128
HB = 64
ROWS = 16
COLS = 8
HALF = 8
LR = 8
LC = 16
CB = 8
PANEL = 1024
f32 = jnp.float32
bf16 = jnp.bfloat16
exact = lax.Precision.HIGHEST
MIB = 2**20
VMEM = 62 * MIB
CHEAP = pl.CostEstimate(flops=2**10, bytes_accessed=2**10, transcendentals=0)


def block_dot(left, right, contract_left=1):
    dims = (((contract_left,), (0,)), ((), ()))
    return lax.dot_general(left, right, dims, preferred_element_type=f32)


def turned_dot(left, right):
    dims = (((1,), (1,)), ((), ()))
    return lax.dot_general(left, right, dims, preferred_element_type=f32)


def exact_dot(left, right, contract_left=1):
    dims = (((contract_left,), (0,)), ((), ()))
    return lax.dot_general(left, right, dims, precision=exact, preferred_element_type=f32)


def split(value):
    high = value.astype(bf16)
    return high, (value - high.astype(f32)).astype(bf16)


def pack_slots(child, table):
    def body(tab, child_ref, out_ref, held, packed, zero, in_sem, out_sem):
        def fetch(i):
            return pltpu.make_async_copy(child_ref.at[i], held.at[i], in_sem.at[i])

        for i in range(CB):
            fetch(i).start()
        zero[...] = jnp.zeros_like(zero)
        for i in range(CB):
            parent = tab[i]
            mine = parent % ROWS
            other = (mine + HALF) % ROWS
            fetch(i).wait()
            for place in range(COLS):
                source = tab[CB + place]
                gain = tab[2 * CB + i * CB + source].astype(f32)
                packed[i, place] = held[i, source] * gain
            pltpu.make_async_copy(packed.at[i], out_ref.at[mine], out_sem.at[i, 0]).start()

            @pl.when(parent < HALF)
            def _():
                pltpu.make_async_copy(packed.at[i], out_ref.at[other], out_sem.at[i, 1]).start()

            @pl.when(parent >= HALF)
            def _():
                pltpu.make_async_copy(zero, out_ref.at[other], out_sem.at[i, 1]).start()

        for i in range(CB):
            for n in range(2):
                pltpu.make_async_copy(zero, out_ref.at[0], out_sem.at[i, n]).wait()

    return pl.pallas_call(
        body,
        in_specs=[
            pl.BlockSpec(memory_space=pltpu.SMEM),
            pl.BlockSpec(memory_space=pl.ANY),
        ],
        out_specs=pl.BlockSpec(memory_space=pl.ANY),
        out_shape=jax.ShapeDtypeStruct((ROWS, COLS, B, B), f32),
        scratch_shapes=[
            pltpu.VMEM((CB, CB, B, B), f32),
            pltpu.VMEM((CB, COLS, B, B), f32),
            pltpu.VMEM((COLS, B, B), f32),
            pltpu.SemaphoreType.DMA((CB,)),
            pltpu.SemaphoreType.DMA((CB, 2)),
        ],
        compiler_params=pltpu.CompilerParams(vmem_limit_bytes=VMEM),
        cost_estimate=CHEAP,
    )(table, child)


def gain_of(code):
    return (code > 0).astype(f32)


def place_of(code):
    return jnp.maximum(code - 1, 0)


NKEYS = LR + 1 + LC


def panel_column(front, arrived, table):
    def body(tab, front_ref, arrived_ref, out_ref, own, got, own_sem, got_sem):
        def fetch(l):
            copies = [pltpu.make_async_copy(front_ref.at[l, 0], own.at[l], own_sem.at[l])]
            for child in range(2):
                base = child * NKEYS
                row = child * HALF + place_of(tab[base + l])
                block = arrived_ref.at[row, place_of(tab[base + LR + 1])]
                copies.append(
                    pltpu.make_async_copy(block, got.at[child, l], got_sem.at[child, l])
                )
            return copies

        for l in range(LR):
            for copy in fetch(l):
                copy.start()
        for l in range(LR):
            for copy in fetch(l):
                copy.wait()
            value = own[l]
            for child in range(2):
                base = child * NKEYS
                value = value + got[child, l] * (
                    gain_of(tab[base + LR + 1]) * gain_of(tab[base + l])
                )
            out_ref[l] = value

    return pl.pallas_call(
        body,
        in_specs=[
            pl.BlockSpec(memory_space=pltpu.SMEM),
            pl.BlockSpec(memory_space=pl.ANY),
            pl.BlockSpec(memory_space=pl.ANY),
        ],
        out_specs=pl.BlockSpec(memory_space=pltpu.VMEM),
        out_shape=jax.ShapeDtypeStruct((LR, B, B), f32),
        scratch_shapes=[
            pltpu.VMEM((LR, B, B), f32),
            pltpu.VMEM((2, LR, B, B), f32),
            pltpu.SemaphoreType.DMA((LR,)),
            pltpu.SemaphoreType.DMA((2, LR)),
        ],
        compiler_params=pltpu.CompilerParams(vmem_limit_bytes=VMEM),
        cost_estimate=CHEAP,
    )(table, front, arrived)


def leading_row(front, received, arrived, table):
    def body(tab, own_ref, recv_ref, first_ref, other_ref, top_ref, lead_ref):
        upper = tab[2 * NKEYS] < HALF
        for m in range(LC):
            value = jnp.where(upper, own_ref[0, m, 0], recv_ref[m])
            for child, ref in ((0, first_ref), (1, other_ref)):
                base = child * NKEYS
                code = tab[base + LR + 1 + m]
                gain = gain_of(code) * gain_of(tab[base + LR])
                value = value + ref[0, place_of(code), 0] * gain
            top_ref[m] = value
        lead_ref[...] = top_ref[0]

    def rows_of(child):
        def pick(step, tab):
            row = child * HALF + place_of(tab[child * NKEYS + LR])
            return row, 0, tab[2 * NKEYS] // HALF, 0, 0

        return pick

    return pl.pallas_call(
        body,
        grid_spec=pltpu.PrefetchScalarGridSpec(
            num_scalar_prefetch=1,
            grid=(1,),
            in_specs=[
                pl.BlockSpec((1, LC, 1, HB, B), lambda step, tab: (0, 0, 0, 0, 0)),
                pl.BlockSpec((LC, HB, B), lambda step, tab: (0, 0, 0)),
                pl.BlockSpec((1, COLS, 1, HB, B), rows_of(0)),
                pl.BlockSpec((1, COLS, 1, HB, B), rows_of(1)),
            ],
            out_specs=[
                pl.BlockSpec((LC, HB, B), lambda step, tab: (0, 0, 0)),
                pl.BlockSpec((HB, B), lambda step, tab: (0, 0)),
            ],
        ),
        out_shape=[
            jax.ShapeDtypeStruct((LC, HB, B), f32),
            jax.ShapeDtypeStruct((HB, B), f32),
        ],
        compiler_params=pltpu.CompilerParams(vmem_limit_bytes=VMEM),
        cost_estimate=CHEAP,
    )(table, front, received, arrived, arrived)


def extend_add(front, arrived, table):
    def body(tab, parent_ref, first_ref, other_ref, out_ref):
        step = pl.program_id(0)
        for m in range(LC):
            value = parent_ref[0, m]
            for child, ref in ((0, first_ref), (1, other_ref)):
                base = child * NKEYS
                code = tab[base + LR + 1 + m]
                gain = gain_of(code) * gain_of(tab[base + step])
                value = value + ref[0, place_of(code)] * gain
            out_ref[0, m] = value

    def rows_of(child):
        return lambda step, tab: (child * HALF + place_of(tab[child * NKEYS + step]), 0, 0, 0)

    return pl.pallas_call(
        body,
        grid_spec=pltpu.PrefetchScalarGridSpec(
            num_scalar_prefetch=1,
            grid=(LR,),
            in_specs=[
                pl.BlockSpec((1, LC, B, B), lambda step, tab: (step, 0, 0, 0)),
                pl.BlockSpec((1, COLS, B, B), rows_of(0)),
                pl.BlockSpec((1, COLS, B, B), rows_of(1)),
            ],
            out_specs=pl.BlockSpec((1, LC, B, B), lambda step, tab: (step, 0, 0, 0)),
        ),
        out_shape=jax.ShapeDtypeStruct((LR, LC, B, B), f32),
        compiler_params=pltpu.CompilerParams(vmem_limit_bytes=VMEM),
        cost_estimate=CHEAP,
    )(table, front, arrived, arrived)


def factor_block(block):
    lane = lax.broadcasted_iota(jnp.int32, (8, B), 1)
    sub = lax.broadcasted_iota(jnp.int32, (8, B), 0)

    def lanes(tile, j):
        return jnp.broadcast_to(tile[:, j : j + 1], (8, B))

    def subs(tile, k):
        return jnp.broadcast_to(tile[k : k + 1, :], (8, B))

    tiles = [block[8 * r : 8 * r + 8, :] for r in range(B // 8)]
    for group in range(B // 8):
        low = 8 * group
        own = [lanes(tiles[group], low + k) for k in range(8)]
        work = tiles[group]
        inside = jnp.logical_and(lane >= low, lane < low + 8)
        upper = []
        for k in range(0, 8, 2):
            n = k + 1
            a, b, c = subs(own[k], k), subs(own[n], k), subs(own[n], n)
            det = 1.0 / (a * c - b * b)
            at_k, at_n = lane == low + k, lane == low + n
            on_k, on_n = sub == k, sub == n
            on = jnp.logical_or(on_k, on_n)
            row_k, row_n = subs(work, k), subs(work, n)
            upper.append(row_k)
            ratio = b * (1.0 / a)
            upper.append(jnp.where(at_k, 0.0, row_n) - ratio * jnp.where(at_k, 1.0, row_k))
            row_k = jnp.where(at_k, 1.0, jnp.where(at_n, 0.0, row_k))
            row_n = jnp.where(at_n, 1.0, jnp.where(at_k, 0.0, row_n))
            new_k = det * (c * row_k - b * row_n)
            new_n = det * (a * row_n - b * row_k)
            coef_k = jnp.where(on_k, -1.0, jnp.where(on_n, 0.0, own[k]))
            coef_n = jnp.where(on_n, -1.0, jnp.where(on_k, 0.0, own[n]))
            clear = jnp.logical_or(jnp.logical_or(at_k, at_n), on)
            work = jnp.where(clear, 0.0, work) - coef_k * new_k - coef_n * new_n
            for m in range(k + 2, 8):
                x, y = subs(own[m], k), subs(own[m], n)
                step = coef_k * (det * (c * x - b * y)) + coef_n * (det * (a * y - b * x))
                own[m] = jnp.where(on, 0.0, own[m]) - step
        solved = [subs(work, k) for k in range(8)]
        rows = upper[0]
        for k in range(1, 8):
            rows = jnp.where(sub == k, upper[k], rows)
        tiles[group] = rows
        for r in range(group + 1, B // 8):
            value = jnp.where(inside, 0.0, tiles[r])
            for k in range(8):
                value = value - lanes(tiles[r], low + k) * solved[k]
            tiles[r] = value
    return jnp.concatenate(tiles, axis=0)


def leading_factor(pieces, where):
    def body(at, *refs):
        piece_refs, (w, diag) = refs[:10], refs[10:]
        for n, ref in enumerate(piece_refs):
            dk, dy = n // 5, (0, 1, 3, 2, 2)[n % 5]
            q = ((at[2] + dy) % 4) * 2 + (at[3] + dk) % 2
            for dx in range(ref.shape[0]):
                x = (at[0] + dx + (2 if n % 5 == 4 else 0)) % 4
                for dz in range(4):
                    g = (x % 2) * 4 + (at[1] + dz) % 4
                    top = pl.multiple_of(g * B + (x // 2) * HB, HB)
                    w[pl.ds(top, HB), pl.ds(pl.multiple_of(q * B, B), B)] = ref[dx, dz]
        row = lax.broadcasted_iota(jnp.int32, (B, B), 0)
        col = lax.broadcasted_iota(jnp.int32, (B, B), 1)

        def step(kb, carry):
            o = pl.multiple_of(kb * B, B)
            f = factor_block(w[pl.ds(o, B), pl.ds(o, B)])
            pivots = jnp.sum(jnp.where(row == col, f, 0.0), axis=1, keepdims=True)
            scale = 1.0 / jnp.sqrt(pivots)
            inverse = jnp.where(row > col, f, (row == col).astype(f32)) * scale
            diag[pl.ds(o, B), :] = jnp.where(row <= col, f, 0.0) * scale
            w[pl.ds(o, B), :] = exact_dot(inverse, w[pl.ds(o, B), :])
            w[pl.ds(o, B), pl.ds(o, B)] = inverse

            @pl.when(kb % 2 == 0)
            def _():
                n = pl.multiple_of(o + B, B)
                w[pl.ds(n, B), pl.ds(o, B)] = jnp.zeros((B, B), f32)
                w[pl.ds(n, B), :] -= exact_dot(w[pl.ds(o, B), pl.ds(n, B)], w[pl.ds(o, B), :], 0)

            for done in range(256, PANEL, 256):

                @pl.when(kb == done // B - 1)
                def _():
                    above = (slice(done - 256, done - B), slice(done - B, done))
                    kept = w[above]
                    w[above] = jnp.zeros((B, B), f32)
                    w[done:, done - 256 : done] = jnp.zeros((PANEL - done, 256), f32)
                    for n in range(done, PANEL, 256):
                        left = w[done - 256 : done, n : n + 256]
                        w[n : n + 256, :] -= exact_dot(left, w[done - 256 : done, :], 0)
                    w[above] = kept

            return carry

        lax.fori_loop(0, PANEL // B, step, 0)

    return pl.pallas_call(
        body,
        in_specs=[pl.BlockSpec(memory_space=pltpu.SMEM)]
        + [pl.BlockSpec(memory_space=pltpu.VMEM)] * 10,
        out_specs=[pl.BlockSpec(memory_space=pltpu.VMEM)] * 2,
        out_shape=[
            jax.ShapeDtypeStruct((PANEL, PANEL), f32),
            jax.ShapeDtypeStruct((PANEL, B), f32),
        ],
        compiler_params=pltpu.CompilerParams(vmem_limit_bytes=VMEM),
        cost_estimate=CHEAP,
    )(where, *pieces)


def panel_solve(rows, w, diag, where):
    def body(at, rows_ref, w_ref, diag_ref, high_ref, low_ref, out_ref, rh, rl, wh, wl, below, bh, bl):
        p, q = at[0], at[1]
        for e in range(COLS):
            for l in range(LR):
                high, low = split(rows_ref[e, l])
                rh[l * B : (l + 1) * B, e * B : (e + 1) * B] = high
                rl[l * B : (l + 1) * B, e * B : (e + 1) * B] = low
        for r in range(0, PANEL, 256):
            shape = (256, r + 256)
            under = (
                lax.broadcasted_iota(jnp.int32, shape, 0) + r
                >= lax.broadcasted_iota(jnp.int32, shape, 1)
            )
            high, low = split(jnp.where(under, w_ref[r : r + 256, : r + 256], 0.0))
            wh[r : r + 256, : r + 256] = high
            wl[r : r + 256, : r + 256] = low
            value = turned_dot(rh[:, : r + 256], high)
            value += turned_dot(rl[:, : r + 256], high)
            value += turned_dot(rh[:, : r + 256], low)
            below[:, r : r + 256] = value
            high, low = split(value)
            bh[:, r : r + 256] = high
            bl[:, r : r + 256] = low
        mine = pl.ds(pl.multiple_of(q * B, B), B)
        for l in range(LR):
            out_ref[l] = below[l * B : (l + 1) * B, mine]

        @pl.when(p < HALF)
        def _():
            over = w_ref[mine, pl.ds(pl.multiple_of((p % HALF) * B, B), B)]
            top = jnp.where(p > q, over, jnp.where(p == q, diag_ref[mine, :], 0.0))
            out_ref[0] = top.T

        for r in range(0, PANEL, 256):
            value = block_dot(bh[:, r:], wh[r:, r : r + 256])
            value += block_dot(bl[:, r:], wh[r:, r : r + 256])
            value += block_dot(bh[:, r:], wl[r:, r : r + 256])
            high, low = split(value)
            high_ref[:, r : r + 256] = high
            low_ref[:, r : r + 256] = low

        @pl.when(p < HALF)
        def _():
            high_ref[:B, :] = jnp.zeros((B, PANEL), bf16)
            low_ref[:B, :] = jnp.zeros((B, PANEL), bf16)

    return pl.pallas_call(
        body,
        in_specs=[pl.BlockSpec(memory_space=pltpu.SMEM)]
        + [pl.BlockSpec(memory_space=pltpu.VMEM)] * 3,
        out_specs=[pl.BlockSpec(memory_space=pltpu.VMEM)] * 3,
        out_shape=[
            jax.ShapeDtypeStruct((PANEL, PANEL), bf16),
            jax.ShapeDtypeStruct((PANEL, PANEL), bf16),
            jax.ShapeDtypeStruct((LR, B, B), f32),
        ],
        scratch_shapes=[
            pltpu.VMEM((PANEL, PANEL), bf16),
            pltpu.VMEM((PANEL, PANEL), bf16),
            pltpu.VMEM((PANEL, PANEL), bf16),
            pltpu.VMEM((PANEL, PANEL), bf16),
            pltpu.VMEM((PANEL, PANEL), f32),
            pltpu.VMEM((PANEL, PANEL), bf16),
            pltpu.VMEM((PANEL, PANEL), bf16),
        ],
        compiler_params=pltpu.CompilerParams(vmem_limit_bytes=VMEM),
        cost_estimate=CHEAP,
    )(where, rows, w, diag)


def trailing_update(assembled, columns, high, low, panel):
    def body(front_ref, col_ref, high_ref, low_ref, panel_ref, out_ref, ch, cl):
        for p in range(ROWS):
            top = (p % HALF) * B + (p // HALF) * HB
            for n in range(2):
                hi, lo = split(col_ref[p, n])
                ch[top : top + HB, n * B : (n + 1) * B] = hi
                cl[top : top + HB, n * B : (n + 1) * B] = lo
        for r in range(0, PANEL, 256):
            value = block_dot(high_ref[r : r + 256, :], ch[...])
            value += block_dot(high_ref[r : r + 256, :], cl[...])
            value += block_dot(low_ref[r : r + 256, :], ch[...])
            for l in range(r // B, r // B + 2):
                for n in range(2):
                    s = l * B - r
                    out_ref[l, n] = front_ref[l, n] - value[s : s + B, n * B : (n + 1) * B]

        @pl.when(pl.program_id(0) == 0)
        def _():
            for l in range(LR):
                out_ref[l, 0] = panel_ref[l]

    blocks = pl.BlockSpec((LR, 2, B, B), lambda step: (0, step, 0, 0))
    whole = pl.BlockSpec((PANEL, PANEL), lambda step: (0, 0))
    return pl.pallas_call(
        body,
        grid=(LC // 2,),
        in_specs=[
            blocks,
            pl.BlockSpec((ROWS, 2, HB, B), lambda step: (0, step, 0, 0)),
            whole,
            whole,
            pl.BlockSpec((LR, B, B), lambda step: (0, 0, 0)),
        ],
        out_specs=blocks,
        out_shape=jax.ShapeDtypeStruct((LR, LC, B, B), f32),
        scratch_shapes=[pltpu.VMEM((PANEL, 256), bf16), pltpu.VMEM((PANEL, 256), bf16)],
        compiler_params=pltpu.CompilerParams(vmem_limit_bytes=VMEM),
        cost_estimate=CHEAP,
    )(assembled, columns, high, low, panel)


def along_x(distance):
    return [(4 * ((x + distance) % 4) + z, 4 * x + z) for x in range(4) for z in range(4)]


def along_z(distance):
    return [(4 * x + (z + distance) % 4, 4 * x + z) for x in range(4) for z in range(4)]


def along_y(distance):
    return [(2 * ((y + distance) % 4) + k, 2 * y + k) for y in range(4) for k in range(2)]


OTHER_CORE = [(q, q ^ 1) for q in range(COLS)]


def shards(parent_front, child_updates, child_mask, child_map):
    p = lax.axis_index("row")
    q = lax.axis_index("col")
    both = ("row", "col")
    front = parent_front.reshape(LR, LC, 2, HB, B)

    own_map = child_map[p // HALF].reshape(CB, CB)
    row_parent = own_map[:, p % HALF]
    col_parent = own_map[:, q]
    index = jnp.arange(CB)
    column = jnp.sum((col_parent[None] % COLS == index[:, None]) * index[None], axis=1)
    source_table = jnp.concatenate([row_parent, column, child_mask.reshape(-1)]).astype(jnp.int32)

    keys = jnp.concatenate(
        [jnp.arange(LR) * ROWS + p, (p % HALF)[None], jnp.arange(LC) * COLS + q]
    )
    hits = child_map[:, None, :] == keys[None, :, None]
    codes = jnp.sum(hits * (jnp.arange(CB * CB) % CB + 1)[None, None], axis=2)
    target_table = jnp.concatenate([codes.reshape(-1), p[None]]).astype(jnp.int32)

    top_other = lax.ppermute(front[0, :, 1], "row", [(i, i + HALF) for i in range(HALF)])

    slots = pack_slots(child_updates, source_table)
    arrived = lax.all_to_all(
        slots.reshape(ROWS * COLS, B, B), both, 0, 0, tiled=True
    ).reshape(ROWS, COLS, B, B)

    target_table, top_other = lax.optimization_barrier((target_table, top_other))
    column = panel_column(parent_front, arrived, target_table)
    panel_rows = lax.all_gather(column, "col", axis=0)

    halves = arrived.reshape(ROWS, COLS, 2, HB, B)
    top, lead = leading_row(front, top_other, halves, target_table)
    columns = lax.all_gather(top, "row", axis=0)

    near = [lead] + [lax.ppermute(lead, "row", along_z(d)) for d in range(1, 4)]
    stacked = jnp.stack(near)
    near = [stacked] + [lax.ppermute(stacked, "row", along_x(d)) for d in range(1, 4)]
    stacked = jnp.stack(near)
    ahead = lax.ppermute(stacked, "col", along_y(1))
    back = lax.ppermute(stacked, "col", along_y(3))
    assembled = extend_add(parent_front, arrived, target_table)
    assembled, ahead, back = lax.optimization_barrier((assembled, ahead, back))
    far = [
        lax.ppermute(ahead[:2], "col", along_y(1)),
        lax.ppermute(back[2:], "col", along_y(3)),
    ]
    near = [stacked, ahead, back] + far
    near = near + [lax.ppermute(piece, "col", OTHER_CORE) for piece in near]

    where = jnp.stack([p // 4, p % 4, q // 2, q % 2]).astype(jnp.int32)
    w, diag = leading_factor(near, where)
    high, low, panel = panel_solve(panel_rows, w, diag, jnp.stack([p, q]).astype(jnp.int32))
    return trailing_update(assembled, columns, high, low, panel)


def solution(mesh):
    in_specs = (P("row", "col", None, None), P("row", "col", None, None), P("row", "col"), P())
    out_specs = P("row", "col", None, None)
    return jax.shard_map(shards, mesh=mesh, in_specs=in_specs, out_specs=out_specs, check_vma=False)
```

```python
import jax
import jax.numpy as jnp
from jax import lax
from jax.experimental import pallas as pl
from jax.experimental.pallas import tpu as pltpu
from jax.sharding import PartitionSpec as P

B = 128
HB = 64
ROWS = 16
COLS = 8
HALF = 8
LR = 8
LC = 16
CB = 8
PANEL = 1024
f32 = jnp.float32
bf16 = jnp.bfloat16
exact = lax.Precision.HIGHEST
MIB = 2**20
VMEM = 62 * MIB
CHEAP = pl.CostEstimate(flops=2**10, bytes_accessed=2**10, transcendentals=0)


def block_dot(left, right, contract_left=1):
    dims = (((contract_left,), (0,)), ((), ()))
    return lax.dot_general(left, right, dims, preferred_element_type=f32)


def exact_dot(left, right, contract_left=1):
    dims = (((contract_left,), (0,)), ((), ()))
    return lax.dot_general(left, right, dims, precision=exact, preferred_element_type=f32)


def split(value):
    high = value.astype(bf16)
    return high, (value - high.astype(f32)).astype(bf16)


def pack_slots(child, table, second):
    def body(tab, child_ref, out_ref, held, packed, zero, in_sem, out_sem):
        halves = (1,) if second else (0, 1)
        size = len(halves)

        def fetch(i, n):
            return pltpu.make_async_copy(
                child_ref.at[i, :, halves[n]], held.at[i, n], in_sem.at[i, n]
            )

        for i in range(CB):
            for n in range(size):
                fetch(i, n).start()
        zero[...] = jnp.zeros_like(zero)
        for i in range(CB):
            parent = tab[i]
            mine = parent % ROWS
            other = (mine + HALF) % ROWS
            for n in range(size):
                fetch(i, n).wait()
                for place in range(COLS):
                    source = tab[CB + place]
                    gain = tab[2 * CB + i * CB + source].astype(f32)
                    packed[i, n, place] = held[i, n, source] * gain
            pltpu.make_async_copy(packed.at[i, 0], out_ref.at[mine], out_sem.at[i, 0]).start()
            if second:
                pltpu.make_async_copy(zero, out_ref.at[other], out_sem.at[i, 1]).start()
            else:

                @pl.when(parent < HALF)
                def _():
                    pltpu.make_async_copy(
                        packed.at[i, 1], out_ref.at[other], out_sem.at[i, 1]
                    ).start()

                @pl.when(parent >= HALF)
                def _():
                    pltpu.make_async_copy(zero, out_ref.at[other], out_sem.at[i, 1]).start()

        for i in range(CB):
            for n in range(2):
                pltpu.make_async_copy(zero, out_ref.at[0], out_sem.at[i, n]).wait()

    size = 1 if second else 2
    return pl.pallas_call(
        body,
        in_specs=[
            pl.BlockSpec(memory_space=pltpu.SMEM),
            pl.BlockSpec(memory_space=pl.ANY),
        ],
        out_specs=pl.BlockSpec(memory_space=pl.ANY),
        out_shape=jax.ShapeDtypeStruct((ROWS, COLS, HB, B), f32),
        scratch_shapes=[
            pltpu.VMEM((CB, size, CB, HB, B), f32),
            pltpu.VMEM((CB, size, COLS, HB, B), f32),
            pltpu.VMEM((COLS, HB, B), f32),
            pltpu.SemaphoreType.DMA((CB, size)),
            pltpu.SemaphoreType.DMA((CB, 2)),
        ],
        compiler_params=pltpu.CompilerParams(vmem_limit_bytes=VMEM),
        cost_estimate=CHEAP,
    )(table, child)


def gain_of(code):
    return (code > 0).astype(f32)


def place_of(code):
    return jnp.maximum(code - 1, 0)


NKEYS = LR + 1 + LC


def leading_row(front, received, arrived, table):
    def body(tab, own_ref, recv_ref, first_ref, other_ref, top_ref, even_ref, odd_ref, lead_ref):
        upper = tab[2 * NKEYS] < HALF
        side = tab[2 * NKEYS] // HALF
        for m in range(LC):
            value = jnp.where(upper, own_ref[0, m, 0], recv_ref[m])
            for child, ref in ((0, first_ref), (1, other_ref)):
                base = child * NKEYS
                code = tab[base + LR + 1 + m]
                gain = gain_of(code) * gain_of(tab[base + LR])
                value = value + ref[0, place_of(code)] * gain
            top_ref[m] = value
        lead_ref[...] = top_ref[0]
        for l in range(LR):
            even_ref[l] = top_ref[2 * l + side]
            odd_ref[l] = top_ref[2 * l + 1 - side]

    def rows_of(child):
        return lambda step, tab: (child * HALF + place_of(tab[child * NKEYS + LR]), 0, 0, 0)

    return pl.pallas_call(
        body,
        grid_spec=pltpu.PrefetchScalarGridSpec(
            num_scalar_prefetch=1,
            grid=(1,),
            in_specs=[
                pl.BlockSpec((1, LC, 1, HB, B), lambda step, tab: (0, 0, 0, 0, 0)),
                pl.BlockSpec((LC, HB, B), lambda step, tab: (0, 0, 0)),
                pl.BlockSpec((1, COLS, HB, B), rows_of(0)),
                pl.BlockSpec((1, COLS, HB, B), rows_of(1)),
            ],
            out_specs=[
                pl.BlockSpec((LC, HB, B), lambda step, tab: (0, 0, 0)),
                pl.BlockSpec((LR, HB, B), lambda step, tab: (0, 0, 0)),
                pl.BlockSpec((LR, HB, B), lambda step, tab: (0, 0, 0)),
                pl.BlockSpec((HB, B), lambda step, tab: (0, 0)),
            ],
        ),
        out_shape=[
            jax.ShapeDtypeStruct((LC, HB, B), f32),
            jax.ShapeDtypeStruct((LR, HB, B), f32),
            jax.ShapeDtypeStruct((LR, HB, B), f32),
            jax.ShapeDtypeStruct((HB, B), f32),
        ],
        compiler_params=pltpu.CompilerParams(vmem_limit_bytes=VMEM),
        cost_estimate=CHEAP,
    )(table, front, received, arrived, arrived)


def extend_add(front, arrived, table, half):
    def body(tab, parent_ref, first_ref, other_ref, out_ref):
        step = pl.program_id(0)
        for m in range(LC):
            value = parent_ref[0, m, 0]
            for child, ref in ((0, first_ref), (1, other_ref)):
                base = child * NKEYS
                code = tab[base + LR + 1 + m]
                gain = gain_of(code) * gain_of(tab[base + step])
                value = value + ref[0, place_of(code)] * gain
            out_ref[0, m] = value

    def rows_of(child):
        return lambda step, tab: (child * HALF + place_of(tab[child * NKEYS + step]), 0, 0, 0)

    return pl.pallas_call(
        body,
        grid_spec=pltpu.PrefetchScalarGridSpec(
            num_scalar_prefetch=1,
            grid=(LR,),
            in_specs=[
                pl.BlockSpec((1, LC, 1, HB, B), lambda step, tab: (step, 0, half, 0, 0)),
                pl.BlockSpec((1, COLS, HB, B), rows_of(0)),
                pl.BlockSpec((1, COLS, HB, B), rows_of(1)),
            ],
            out_specs=pl.BlockSpec((1, LC, HB, B), lambda step, tab: (step, 0, 0, 0)),
        ),
        out_shape=jax.ShapeDtypeStruct((LR, LC, HB, B), f32),
        compiler_params=pltpu.CompilerParams(vmem_limit_bytes=VMEM),
        cost_estimate=CHEAP,
    )(table, front, arrived, arrived)


def factor_block(block):
    lane = lax.broadcasted_iota(jnp.int32, (8, B), 1)
    sub = lax.broadcasted_iota(jnp.int32, (8, B), 0)

    def lanes(tile, j):
        return jnp.broadcast_to(tile[:, j : j + 1], (8, B))

    def subs(tile, k):
        return jnp.broadcast_to(tile[k : k + 1, :], (8, B))

    tiles = [block[8 * r : 8 * r + 8, :] for r in range(B // 8)]
    for group in range(B // 8):
        low = 8 * group
        own = [lanes(tiles[group], low + k) for k in range(8)]
        work = tiles[group]
        inside = jnp.logical_and(lane >= low, lane < low + 8)
        upper = []
        for k in range(0, 8, 2):
            n = k + 1
            a, b, c = subs(own[k], k), subs(own[n], k), subs(own[n], n)
            det = 1.0 / (a * c - b * b)
            at_k, at_n = lane == low + k, lane == low + n
            on_k, on_n = sub == k, sub == n
            on = jnp.logical_or(on_k, on_n)
            row_k, row_n = subs(work, k), subs(work, n)
            upper.append(row_k)
            ratio = b * (1.0 / a)
            upper.append(jnp.where(at_k, 0.0, row_n) - ratio * jnp.where(at_k, 1.0, row_k))
            row_k = jnp.where(at_k, 1.0, jnp.where(at_n, 0.0, row_k))
            row_n = jnp.where(at_n, 1.0, jnp.where(at_k, 0.0, row_n))
            new_k = det * (c * row_k - b * row_n)
            new_n = det * (a * row_n - b * row_k)
            coef_k = jnp.where(on_k, -1.0, jnp.where(on_n, 0.0, own[k]))
            coef_n = jnp.where(on_n, -1.0, jnp.where(on_k, 0.0, own[n]))
            clear = jnp.logical_or(jnp.logical_or(at_k, at_n), on)
            work = jnp.where(clear, 0.0, work) - coef_k * new_k - coef_n * new_n
            for m in range(k + 2, 8):
                x, y = subs(own[m], k), subs(own[m], n)
                step = coef_k * (det * (c * x - b * y)) + coef_n * (det * (a * y - b * x))
                own[m] = jnp.where(on, 0.0, own[m]) - step
        solved = [subs(work, k) for k in range(8)]
        rows = upper[0]
        for k in range(1, 8):
            rows = jnp.where(sub == k, upper[k], rows)
        tiles[group] = rows
        for r in range(group + 1, B // 8):
            value = jnp.where(inside, 0.0, tiles[r])
            for k in range(8):
                value = value - lanes(tiles[r], low + k) * solved[k]
            tiles[r] = value
    return jnp.concatenate(tiles, axis=0)


def factor_and_solve(pieces, where):
    def origin(at, n):
        dk, dy = n // 5, (0, 1, 3, 2, 2)[n % 5]
        return ((at[2] + dy) % 4) * 2 + (at[3] + dk) % 2

    def body(at, *refs):
        lead_refs, rows_refs, refs = refs[:10], refs[10:20], refs[20:]
        high_ref, low_ref, out_ref, w, diag, rows, gh, gl, wh, wl, below, bh, bl, sem = refs
        p = at[0] * 4 + at[1]
        q = at[2] * 2 + at[3]
        side = p // HALF
        copies = []
        for n, ref in enumerate(rows_refs):
            e = origin(at, n) ^ (p % HALF)
            for half in range(ref.shape[0]):
                order = 1 if n % 5 == 4 else half
                copies.append(
                    pltpu.make_async_copy(ref.at[half, 1], rows.at[e, order], sem.at[e, order])
                )
        for copy in copies:
            copy.start()
        for n, ref in enumerate(lead_refs):
            e = origin(at, n)
            for half in range(ref.shape[0]):
                for place in range(LR):
                    dx = half * 2 + place // 4 + (2 if n % 5 == 4 else 0)
                    x, z = (at[0] + dx) % 4, (at[1] + place) % 4
                    g = (x % 2) * 4 + z
                    top = pl.multiple_of(g * B + (x // 2) * HB, HB)
                    w[pl.ds(top, HB), pl.ds(pl.multiple_of(e * B, B), B)] = ref[half, 0, place]
        row = lax.broadcasted_iota(jnp.int32, (B, B), 0)
        col = lax.broadcasted_iota(jnp.int32, (B, B), 1)
        def step(kb, carry):
            o = pl.multiple_of(kb * B, B)
            f = factor_block(w[pl.ds(o, B), pl.ds(o, B)])
            pivots = jnp.sum(jnp.where(row == col, f, 0.0), axis=1, keepdims=True)
            scale = 1.0 / jnp.sqrt(pivots)
            inverse = jnp.where(row > col, f, (row == col).astype(f32)) * scale
            diag[pl.ds(o, B), :] = jnp.where(row <= col, f, 0.0) * scale
            w[pl.ds(o, B), :] = exact_dot(inverse, w[pl.ds(o, B), :])
            w[pl.ds(o, B), pl.ds(o, B)] = inverse

            @pl.when(kb % 2 == 0)
            def _():
                n = pl.multiple_of(o + B, B)
                w[pl.ds(n, B), pl.ds(o, B)] = jnp.zeros((B, B), f32)
                w[pl.ds(n, B), :] -= exact_dot(w[pl.ds(o, B), pl.ds(n, B)], w[pl.ds(o, B), :], 0)

            for done in range(256, PANEL, 256):

                @pl.when(kb == done // B - 1)
                def _():
                    above = (slice(done - 256, done - B), slice(done - B, done))
                    kept = w[above]
                    w[above] = jnp.zeros((B, B), f32)
                    w[done:, done - 256 : done] = jnp.zeros((PANEL - done, 256), f32)
                    for n in range(done, PANEL, 256):
                        left = w[done - 256 : done, n : n + 256]
                        w[n : n + 256, :] -= exact_dot(left, w[done - 256 : done, :], 0)
                    w[above] = kept

            return carry

        lax.fori_loop(0, PANEL // B, step, 0)

        for copy in copies:
            copy.wait()
        for e in range(COLS):
            for order in range(2):
                half = side if order == 0 else 1 - side
                top = pl.multiple_of(e * B + half * HB, HB)
                for l in range(LR):
                    high, low = split(rows[e, order, l])
                    gh[pl.ds(top, HB), l * B : (l + 1) * B] = high
                    gl[pl.ds(top, HB), l * B : (l + 1) * B] = low
        for r in range(0, PANEL, 256):
            shape = (256, r + 256)
            under = (
                lax.broadcasted_iota(jnp.int32, shape, 0) + r
                >= lax.broadcasted_iota(jnp.int32, shape, 1)
            )
            high, low = split(jnp.where(under, w[r : r + 256, : r + 256], 0.0))
            wh[r : r + 256, : r + 256] = high
            wl[r : r + 256, : r + 256] = low
            value = block_dot(high, gh[: r + 256, :])
            value += block_dot(high, gl[: r + 256, :])
            value += block_dot(low, gh[: r + 256, :])
            for l in range(LR):
                for n in range(0, 256, B):
                    tile = value[n : n + B, l * B : (l + 1) * B].T
                    high, low = split(tile)
                    place = (slice(l * B, (l + 1) * B), slice(r + n, r + n + B))
                    below[place] = tile
                    bh[place] = high
                    bl[place] = low
        mine = pl.ds(pl.multiple_of(q * B, B), B)
        for l in range(LR):
            out_ref[l] = below[l * B : (l + 1) * B, mine]

        @pl.when(p < HALF)
        def _():
            over = w[mine, pl.ds(pl.multiple_of((p % HALF) * B, B), B)]
            top = jnp.where(p > q, over, jnp.where(p == q, diag[mine, :], 0.0))
            out_ref[0] = top.T

        for r in range(0, PANEL, 256):
            value = block_dot(bh[:, r:], wh[r:, r : r + 256])
            value += block_dot(bl[:, r:], wh[r:, r : r + 256])
            value += block_dot(bh[:, r:], wl[r:, r : r + 256])
            high, low = split(value)
            high_ref[:, r : r + 256] = high
            low_ref[:, r : r + 256] = low

        @pl.when(p < HALF)
        def _():
            high_ref[:B, :] = jnp.zeros((B, PANEL), bf16)
            low_ref[:B, :] = jnp.zeros((B, PANEL), bf16)

    whole = pl.BlockSpec((PANEL, PANEL), lambda step: (0, 0))
    return pl.pallas_call(
        body,
        grid=(1,),
        in_specs=[pl.BlockSpec(memory_space=pltpu.SMEM)]
        + [
            pl.BlockSpec((piece.shape[0], 1, LR, HB, B), lambda step: (0, 0, 0, 0, 0))
            for piece in pieces
        ]
        + [pl.BlockSpec(memory_space=pl.ANY)] * 10,
        out_specs=[whole, whole, pl.BlockSpec((LR, B, B), lambda step: (0, 0, 0))],
        out_shape=[
            jax.ShapeDtypeStruct((PANEL, PANEL), bf16),
            jax.ShapeDtypeStruct((PANEL, PANEL), bf16),
            jax.ShapeDtypeStruct((LR, B, B), f32),
        ],
        scratch_shapes=[
            pltpu.VMEM((PANEL, PANEL), f32),
            pltpu.VMEM((PANEL, B), f32),
            pltpu.VMEM((COLS, 2, LR, HB, B), f32),
            pltpu.VMEM((PANEL, PANEL), bf16),
            pltpu.VMEM((PANEL, PANEL), bf16),
            pltpu.VMEM((PANEL, PANEL), bf16),
            pltpu.VMEM((PANEL, PANEL), bf16),
            pltpu.VMEM((PANEL, PANEL), f32),
            pltpu.VMEM((PANEL, PANEL), bf16),
            pltpu.VMEM((PANEL, PANEL), bf16),
            pltpu.SemaphoreType.DMA((COLS, 2)),
        ],
        compiler_params=pltpu.CompilerParams(vmem_limit_bytes=VMEM),
        cost_estimate=CHEAP,
    )(where, *pieces, *pieces)


def trailing_update(table, upper, front, second, columns, high, low, panel):
    steps = LC // 2

    def body(tab, upper_ref, front_ref, second_ref, col_ref, high_ref, low_ref, panel_ref, out_ref,
             ch, cl, got, sem):
        step = pl.program_id(0)
        slot = step % 2

        def fetch(step, slot):
            for child in range(2):
                base = child * NKEYS
                for l in range(LR):
                    source = child * HALF + place_of(tab[base + l])
                    for n in range(2):
                        place = place_of(tab[base + LR + 1 + 2 * step + n])
                        pltpu.make_async_copy(
                            second_ref.at[source, place], got.at[slot, child, l, n], sem.at[slot]
                        ).start()

        @pl.when(step == 0)
        def _():
            fetch(step, slot)

        @pl.when(step + 1 < steps)
        def _():
            fetch(step + 1, 1 - slot)

        for p in range(ROWS):
            top = (p % HALF) * B + (p // HALF) * HB
            for n in range(2):
                hi, lo = split(col_ref[p, n])
                ch[top : top + HB, n * B : (n + 1) * B] = hi
                cl[top : top + HB, n * B : (n + 1) * B] = lo
        pltpu.make_async_copy(got.at[slot], got.at[slot], sem.at[slot]).wait()
        for r in range(0, PANEL, 256):
            value = block_dot(high_ref[r : r + 256, :], ch[...])
            value += block_dot(high_ref[r : r + 256, :], cl[...])
            value += block_dot(low_ref[r : r + 256, :], ch[...])
            for l in range(r // B, r // B + 2):
                for n in range(2):
                    s = l * B - r
                    cols = slice(n * B, (n + 1) * B)
                    out_ref[l, n, :HB] = upper_ref[l, n] - value[s : s + HB, cols]
                    total = front_ref[l, n, 0]
                    for child in range(2):
                        base = child * NKEYS
                        gain = gain_of(tab[base + LR + 1 + 2 * step + n]) * gain_of(tab[base + l])
                        total = total + got[slot, child, l, n] * gain
                    out_ref[l, n, HB:] = total - value[s + HB : s + B, cols]

        @pl.when(step == 0)
        def _():
            for l in range(LR):
                out_ref[l, 0] = panel_ref[l]

    whole = pl.BlockSpec((PANEL, PANEL), lambda step, tab: (0, 0))
    return pl.pallas_call(
        body,
        grid_spec=pltpu.PrefetchScalarGridSpec(
            num_scalar_prefetch=1,
            grid=(steps,),
            in_specs=[
                pl.BlockSpec((LR, 2, HB, B), lambda step, tab: (0, step, 0, 0)),
                pl.BlockSpec((LR, 2, 1, HB, B), lambda step, tab: (0, step, 1, 0, 0)),
                pl.BlockSpec(memory_space=pl.ANY),
                pl.BlockSpec((ROWS, 2, HB, B), lambda step, tab: (0, step, 0, 0)),
                whole,
                whole,
                pl.BlockSpec((LR, B, B), lambda step, tab: (0, 0, 0)),
            ],
            out_specs=pl.BlockSpec((LR, 2, B, B), lambda step, tab: (0, step, 0, 0)),
            scratch_shapes=[
                pltpu.VMEM((PANEL, 256), bf16),
                pltpu.VMEM((PANEL, 256), bf16),
                pltpu.VMEM((2, 2, LR, 2, HB, B), f32),
                pltpu.SemaphoreType.DMA((2,)),
            ],
        ),
        out_shape=jax.ShapeDtypeStruct((LR, LC, B, B), f32),
        compiler_params=pltpu.CompilerParams(vmem_limit_bytes=VMEM),
        cost_estimate=CHEAP,
    )(table, upper, front, second, columns, high, low, panel)


def along_x(distance):
    return [(4 * ((x + distance) % 4) + z, 4 * x + z) for x in range(4) for z in range(4)]


def along_z(distance):
    return [(4 * x + (z + distance) % 4, 4 * x + z) for x in range(4) for z in range(4)]


def along_y(distance):
    return [(2 * ((y + distance) % 4) + k, 2 * y + k) for y in range(4) for k in range(2)]


OTHER_CORE = [(q, q ^ 1) for q in range(COLS)]


def transposed(same):
    pairs = []
    for p in range(ROWS):
        for q in range(COLS):
            side = p // HALF if same else 1 - p // HALF
            pairs.append((p * COLS + q, (q + HALF * side) * COLS + (p % HALF ^ q)))
    return pairs


def shards(parent_front, child_updates, child_mask, child_map):
    p = lax.axis_index("row")
    q = lax.axis_index("col")
    both = ("row", "col")
    front = parent_front.reshape(LR, LC, 2, HB, B)
    child = child_updates.reshape(CB, CB, 2, HB, B)

    own_map = child_map[p // HALF].reshape(CB, CB)
    row_parent = own_map[:, p % HALF]
    col_parent = own_map[:, q]
    index = jnp.arange(CB)
    column = jnp.sum((col_parent[None] % COLS == index[:, None]) * index[None], axis=1)
    source_table = jnp.concatenate([row_parent, column, child_mask.reshape(-1)]).astype(jnp.int32)

    keys = jnp.concatenate(
        [jnp.arange(LR) * ROWS + p, (p % HALF)[None], jnp.arange(LC) * COLS + q]
    )
    hits = child_map[:, None, :] == keys[None, :, None]
    codes = jnp.sum(hits * (jnp.arange(CB * CB) % CB + 1)[None, None], axis=2)
    target_table = jnp.concatenate([codes.reshape(-1), p[None]]).astype(jnp.int32)

    top_other = lax.ppermute(front[0, :, 1], "row", [(i, i + HALF) for i in range(HALF)])

    first = pack_slots(child, source_table, False)
    first = lax.all_to_all(
        first.reshape(ROWS * COLS, HB, B), both, 0, 0, tiled=True
    ).reshape(ROWS, COLS, HB, B)
    second = pack_slots(child, source_table, True)

    first, second = lax.optimization_barrier((first, second))
    target_table, top_other = lax.optimization_barrier((target_table, top_other))
    top, even, odd, lead = leading_row(front, top_other, first, target_table)

    turned = [
        lax.ppermute(even, both, transposed(True)),
        lax.ppermute(odd, both, transposed(False)),
    ]
    near = [lead] + [lax.ppermute(lead, "row", along_z(d)) for d in range(1, 4)]
    stacked = jnp.stack(near)
    near = [stacked] + [lax.ppermute(stacked, "row", along_x(d)) for d in range(1, 4)]
    packed = jnp.stack(
        [jnp.concatenate(near[:2]), turned[0], jnp.concatenate(near[2:]), turned[1]]
    ).reshape(2, 2, LR, HB, B)
    top, packed = lax.optimization_barrier((top, packed))

    columns = lax.all_gather(top, "row", axis=0)

    ahead = lax.ppermute(packed, "col", along_y(1))
    back = lax.ppermute(packed, "col", along_y(3))
    upper = extend_add(front, first, target_table, 0)
    upper, ahead, back = lax.optimization_barrier((upper, ahead, back))
    far = [
        lax.ppermute(ahead[:1], "col", along_y(1)),
        lax.ppermute(back[1:], "col", along_y(3)),
    ]
    second, far[0], far[1] = lax.optimization_barrier((second, far[0], far[1]))
    near = [packed, ahead, back] + far
    near = near + [lax.ppermute(piece, "col", OTHER_CORE) for piece in near]

    second = lax.all_to_all(
        second.reshape(ROWS * COLS, HB, B), both, 0, 0, tiled=True
    ).reshape(ROWS, COLS, HB, B)

    where = jnp.stack([p // 4, p % 4, q // 2, q % 2]).astype(jnp.int32)
    high, low, panel = factor_and_solve(near, where)
    high, columns = lax.optimization_barrier((high, columns))
    return trailing_update(target_table, upper, front, second, columns, high, low, panel)


def solution(mesh):
    in_specs = (P("row", "col", None, None), P("row", "col", None, None), P("row", "col"), P())
    out_specs = P("row", "col", None, None)
    return jax.shard_map(shards, mesh=mesh, in_specs=in_specs, out_specs=out_specs, check_vma=False)
```

```python
import jax
import jax.numpy as jnp
from jax import lax
from jax.experimental import pallas as pl
from jax.experimental.pallas import tpu as pltpu
from jax.sharding import PartitionSpec as P

B = 128
HB = 64
ROWS = 16
COLS = 8
HALF = 8
LR = 8
LC = 16
CB = 8
PANEL = 1024
f32 = jnp.float32
bf16 = jnp.bfloat16
exact = lax.Precision.HIGHEST
MIB = 2**20
VMEM = 62 * MIB
CHEAP = pl.CostEstimate(flops=2**10, bytes_accessed=2**10, transcendentals=0)


def block_dot(left, right, contract_left=1):
    dims = (((contract_left,), (0,)), ((), ()))
    return lax.dot_general(left, right, dims, preferred_element_type=f32)


def exact_dot(left, right, contract_left=1):
    dims = (((contract_left,), (0,)), ((), ()))
    return lax.dot_general(left, right, dims, precision=exact, preferred_element_type=f32)


def split(value):
    high = value.astype(bf16)
    return high, (value - high.astype(f32)).astype(bf16)


def pack_slots(child, table, second):
    def body(tab, child_ref, out_ref, held, packed, zero, in_sem, out_sem):
        halves = (1,) if second else (0, 1)
        size = len(halves)

        def fetch(i, n):
            return pltpu.make_async_copy(
                child_ref.at[i, :, halves[n]], held.at[i, n], in_sem.at[i, n]
            )

        def pack(i, n):
            fetch(i, n).wait()
            for place in range(COLS):
                source = tab[CB + place]
                gain = tab[2 * CB + i * CB + source].astype(f32)
                packed[i, n, place] = held[i, n, source] * gain

        for i in range(CB):
            fetch(i, 0).start()
        if not second:
            for i in range(CB):

                @pl.when(tab[i] < HALF)
                def _():
                    fetch(i, 1).start()

        zero[...] = jnp.zeros_like(zero)
        for i in range(CB):
            parent = tab[i]
            mine = parent % ROWS
            other = (mine + HALF) % ROWS
            pack(i, 0)
            pltpu.make_async_copy(packed.at[i, 0], out_ref.at[mine], out_sem.at[i, 0]).start()
            if second:
                pltpu.make_async_copy(zero, out_ref.at[other], out_sem.at[i, 1]).start()
            else:

                @pl.when(parent < HALF)
                def _():
                    pack(i, 1)
                    pltpu.make_async_copy(
                        packed.at[i, 1], out_ref.at[other], out_sem.at[i, 1]
                    ).start()

                @pl.when(parent >= HALF)
                def _():
                    pltpu.make_async_copy(zero, out_ref.at[other], out_sem.at[i, 1]).start()

        for i in range(CB):
            for n in range(2):
                pltpu.make_async_copy(zero, out_ref.at[0], out_sem.at[i, n]).wait()

    size = 1 if second else 2
    return pl.pallas_call(
        body,
        in_specs=[
            pl.BlockSpec(memory_space=pltpu.SMEM),
            pl.BlockSpec(memory_space=pl.ANY),
        ],
        out_specs=pl.BlockSpec(memory_space=pl.ANY),
        out_shape=jax.ShapeDtypeStruct((ROWS, COLS, HB, B), f32),
        scratch_shapes=[
            pltpu.VMEM((CB, size, CB, HB, B), f32),
            pltpu.VMEM((CB, size, COLS, HB, B), f32),
            pltpu.VMEM((COLS, HB, B), f32),
            pltpu.SemaphoreType.DMA((CB, size)),
            pltpu.SemaphoreType.DMA((CB, 2)),
        ],
        compiler_params=pltpu.CompilerParams(vmem_limit_bytes=VMEM),
        cost_estimate=CHEAP,
    )(table, child)


def gain_of(code):
    return (code > 0).astype(f32)


def place_of(code):
    return jnp.maximum(code - 1, 0)


NKEYS = LR + 1 + LC


def leading_row(front, received, arrived, table):
    def body(tab, own_ref, recv_ref, first_ref, other_ref, top_ref, even_ref, odd_ref, lead_ref):
        upper = tab[2 * NKEYS] < HALF
        side = tab[2 * NKEYS] // HALF
        for m in range(LC):
            value = jnp.where(upper, own_ref[0, m, 0], recv_ref[m])
            for child, ref in ((0, first_ref), (1, other_ref)):
                base = child * NKEYS
                code = tab[base + LR + 1 + m]
                gain = gain_of(code) * gain_of(tab[base + LR])
                value = value + ref[0, place_of(code)] * gain
            top_ref[m] = value
        lead_ref[...] = top_ref[0]
        for l in range(LR):
            even_ref[l] = top_ref[2 * l + side]
            odd_ref[l] = top_ref[2 * l + 1 - side]

    def rows_of(child):
        return lambda step, tab: (child * HALF + place_of(tab[child * NKEYS + LR]), 0, 0, 0)

    return pl.pallas_call(
        body,
        grid_spec=pltpu.PrefetchScalarGridSpec(
            num_scalar_prefetch=1,
            grid=(1,),
            in_specs=[
                pl.BlockSpec((1, LC, 1, HB, B), lambda step, tab: (0, 0, 0, 0, 0)),
                pl.BlockSpec((LC, HB, B), lambda step, tab: (0, 0, 0)),
                pl.BlockSpec((1, COLS, HB, B), rows_of(0)),
                pl.BlockSpec((1, COLS, HB, B), rows_of(1)),
            ],
            out_specs=[
                pl.BlockSpec((LC, HB, B), lambda step, tab: (0, 0, 0)),
                pl.BlockSpec((LR, HB, B), lambda step, tab: (0, 0, 0)),
                pl.BlockSpec((LR, HB, B), lambda step, tab: (0, 0, 0)),
                pl.BlockSpec((HB, B), lambda step, tab: (0, 0)),
            ],
        ),
        out_shape=[
            jax.ShapeDtypeStruct((LC, HB, B), f32),
            jax.ShapeDtypeStruct((LR, HB, B), f32),
            jax.ShapeDtypeStruct((LR, HB, B), f32),
            jax.ShapeDtypeStruct((HB, B), f32),
        ],
        compiler_params=pltpu.CompilerParams(vmem_limit_bytes=VMEM),
        cost_estimate=CHEAP,
    )(table, front, received, arrived, arrived)


def extend_add(front, arrived, table, half):
    def body(tab, parent_ref, first_ref, other_ref, out_ref):
        step = pl.program_id(0)
        for m in range(LC):
            value = parent_ref[0, m, 0]
            for child, ref in ((0, first_ref), (1, other_ref)):
                base = child * NKEYS
                code = tab[base + LR + 1 + m]
                gain = gain_of(code) * gain_of(tab[base + step])
                value = value + ref[0, place_of(code)] * gain
            out_ref[0, m] = value

    def rows_of(child):
        return lambda step, tab: (child * HALF + place_of(tab[child * NKEYS + step]), 0, 0, 0)

    return pl.pallas_call(
        body,
        grid_spec=pltpu.PrefetchScalarGridSpec(
            num_scalar_prefetch=1,
            grid=(LR,),
            in_specs=[
                pl.BlockSpec((1, LC, 1, HB, B), lambda step, tab: (step, 0, half, 0, 0)),
                pl.BlockSpec((1, COLS, HB, B), rows_of(0)),
                pl.BlockSpec((1, COLS, HB, B), rows_of(1)),
            ],
            out_specs=pl.BlockSpec((1, LC, HB, B), lambda step, tab: (step, 0, 0, 0)),
        ),
        out_shape=jax.ShapeDtypeStruct((LR, LC, HB, B), f32),
        compiler_params=pltpu.CompilerParams(vmem_limit_bytes=VMEM),
        cost_estimate=CHEAP,
    )(table, front, arrived, arrived)


def factor_block(block):
    lane = lax.broadcasted_iota(jnp.int32, (8, B), 1)
    sub = lax.broadcasted_iota(jnp.int32, (8, B), 0)

    def lanes(tile, j):
        return jnp.broadcast_to(tile[:, j : j + 1], (8, B))

    def subs(tile, k):
        return jnp.broadcast_to(tile[k : k + 1, :], (8, B))

    tiles = [block[8 * r : 8 * r + 8, :] for r in range(B // 8)]
    for group in range(B // 8):
        low = 8 * group
        own = [lanes(tiles[group], low + k) for k in range(8)]
        work = tiles[group]
        inside = jnp.logical_and(lane >= low, lane < low + 8)
        upper = []
        for k in range(0, 8, 2):
            n = k + 1
            a, b, c = subs(own[k], k), subs(own[n], k), subs(own[n], n)
            det = 1.0 / (a * c - b * b)
            at_k, at_n = lane == low + k, lane == low + n
            on_k, on_n = sub == k, sub == n
            on = jnp.logical_or(on_k, on_n)
            row_k, row_n = subs(work, k), subs(work, n)
            upper.append(row_k)
            ratio = b * (1.0 / a)
            upper.append(jnp.where(at_k, 0.0, row_n) - ratio * jnp.where(at_k, 1.0, row_k))
            row_k = jnp.where(at_k, 1.0, jnp.where(at_n, 0.0, row_k))
            row_n = jnp.where(at_n, 1.0, jnp.where(at_k, 0.0, row_n))
            new_k = c * row_k - b * row_n
            new_n = a * row_n - b * row_k
            coef_k = jnp.where(on_k, -1.0, jnp.where(on_n, 0.0, own[k]))
            coef_n = jnp.where(on_n, -1.0, jnp.where(on_k, 0.0, own[n]))
            clear = jnp.logical_or(jnp.logical_or(at_k, at_n), on)
            work = jnp.where(clear, 0.0, work) - det * (coef_k * new_k + coef_n * new_n)
            for m in range(k + 2, 8):
                x, y = subs(own[m], k), subs(own[m], n)
                step = coef_k * (c * x - b * y) + coef_n * (a * y - b * x)
                own[m] = jnp.where(on, 0.0, own[m]) - det * step
        solved = [subs(work, k) for k in range(8)]
        rows = upper[0]
        for k in range(1, 8):
            rows = jnp.where(sub == k, upper[k], rows)
        tiles[group] = rows
        for r in range(group + 1, B // 8):
            value = jnp.where(inside, 0.0, tiles[r])
            for k in range(8):
                value = value - lanes(tiles[r], low + k) * solved[k]
            tiles[r] = value
    return jnp.concatenate(tiles, axis=0)


def factor_and_solve(pieces):
    def origin(at, n):
        dk, dy = n // 5, (0, 1, 3, 2, 2)[n % 5]
        return ((at[2] + dy) % 4) * 2 + (at[3] + dk) % 2

    def body(*refs):
        lead_refs, rows_refs, refs = refs[:10], refs[10:20], refs[20:]
        high_ref, low_ref, out_ref, w, diag, rows, gh, gl, wh, wl, below, bh, bl = refs[:13]
        yh, yl, sem, out_sem = refs[13:]
        p = lax.axis_index("row")
        q = lax.axis_index("col")
        at = (p // 4, p % 4, q // 2, q % 2)
        side = p // HALF
        copies = []
        for n, ref in enumerate(rows_refs):
            e = origin(at, n) ^ (p % HALF)
            for half in range(ref.shape[0]):
                order = 1 if n % 5 == 4 else half
                copies.append(
                    pltpu.make_async_copy(ref.at[half, 1], rows.at[e, order], sem.at[e, order])
                )
        for copy in copies:
            copy.start()
        for n, ref in enumerate(lead_refs):
            e = origin(at, n)
            for half in range(ref.shape[0]):
                for place in range(LR):
                    dx = half * 2 + place // 4 + (2 if n % 5 == 4 else 0)
                    x, z = (at[0] + dx) % 4, (at[1] + place) % 4
                    g = (x % 2) * 4 + z
                    top = pl.multiple_of(g * B + (x // 2) * HB, HB)
                    w[pl.ds(top, HB), pl.ds(pl.multiple_of(e * B, B), B)] = ref[half, 0, place]
        row = lax.broadcasted_iota(jnp.int32, (B, B), 0)
        col = lax.broadcasted_iota(jnp.int32, (B, B), 1)
        count = PANEL // B

        def span(first, last=None):
            return slice(first * B, (first + 1 if last is None else last) * B)

        block = w[span(0), span(0)]
        inverse = None
        for k in range(count):
            f = factor_block(block)
            if k:
                done = k - 1
                right = span(k, count)
                w[span(done), right] = exact_dot(inverse, w[span(done), right])
                if done:
                    left = span(0, done)
                    w[span(done), left] = exact_dot(inverse, w[span(done), left])
                w[span(done), span(done)] = inverse
                for i in range(k, count, 2):
                    rows_now = span(i, min(i + 2, count))
                    cols_now = span(i, count)
                    w[rows_now, cols_now] -= exact_dot(
                        w[span(done), rows_now], w[span(done), cols_now], 0
                    )
                change = exact_dot(w[span(done), right], w[span(done), span(0, k)], 0)
                if done:
                    w[right, span(0, done)] -= change[:, : done * B]
                w[right, span(done)] = -change[:, done * B :]
            pivots = jnp.sum(jnp.where(row == col, f, 0.0), axis=1, keepdims=True)
            scale = 1.0 / jnp.sqrt(pivots)
            inverse = jnp.where(row > col, f, (row == col).astype(f32)) * scale
            diag[span(k), :] = jnp.where(row <= col, f, 0.0) * scale
            if k + 1 < count:
                above = exact_dot(inverse, w[span(k), span(k + 1)])
                block = w[span(k + 1), span(k + 1)] - exact_dot(above, above, 0)
        last = span(count - 1)
        w[last, : PANEL - B] = exact_dot(inverse, w[last, : PANEL - B])
        w[last, last] = inverse

        for copy in copies:
            copy.wait()
        for e in range(COLS):
            for order in range(2):
                half = side if order == 0 else 1 - side
                top = pl.multiple_of(e * B + half * HB, HB)
                for l in range(LR):
                    high, low = split(rows[e, order, l])
                    gh[pl.ds(top, HB), l * B : (l + 1) * B] = high
                    gl[pl.ds(top, HB), l * B : (l + 1) * B] = low
        for r in range(0, PANEL, 256):
            shape = (256, r + 256)
            under = (
                lax.broadcasted_iota(jnp.int32, shape, 0) + r
                >= lax.broadcasted_iota(jnp.int32, shape, 1)
            )
            high, low = split(jnp.where(under, w[r : r + 256, : r + 256], 0.0))
            wh[r : r + 256, : r + 256] = high
            wl[r : r + 256, : r + 256] = low
            value = block_dot(high, gh[: r + 256, :])
            value += block_dot(high, gl[: r + 256, :])
            value += block_dot(low, gh[: r + 256, :])
            for l in range(LR):
                for n in range(0, 256, B):
                    tile = value[n : n + B, l * B : (l + 1) * B].T
                    high, low = split(tile)
                    place = (slice(l * B, (l + 1) * B), slice(r + n, r + n + B))
                    below[place] = tile
                    bh[place] = high
                    bl[place] = low
        mine = pl.ds(pl.multiple_of(q * B, B), B)
        for l in range(LR):
            out_ref[l] = below[l * B : (l + 1) * B, mine]

        @pl.when(p < HALF)
        def _():
            over = w[mine, pl.ds(pl.multiple_of((p % HALF) * B, B), B)]
            top = jnp.where(p > q, over, jnp.where(p == q, diag[mine, :], 0.0))
            out_ref[0] = top.T

        @pl.when(p < HALF)
        def _():
            bh[:B, :] = jnp.zeros((B, PANEL), bf16)
            bl[:B, :] = jnp.zeros((B, PANEL), bf16)

        sends = []
        for n, r in enumerate(range(0, PANEL, 256)):
            cols = slice(r, r + 256)
            value = block_dot(bh[:, r:], wh[r:, cols])
            value += block_dot(bl[:, r:], wh[r:, cols])
            value += block_dot(bh[:, r:], wl[r:, cols])
            yh[:, cols], yl[:, cols] = split(value)
            for m, (held, ref) in enumerate(((yh, high_ref), (yl, low_ref))):
                sends.append(
                    pltpu.make_async_copy(held.at[:, cols], ref.at[:, cols], out_sem.at[n, m])
                )
                sends[-1].start()
        for send in sends:
            send.wait()

    anywhere = pl.BlockSpec(memory_space=pl.ANY)
    return pl.pallas_call(
        body,
        grid=(1,),
        in_specs=[
            pl.BlockSpec((piece.shape[0], 1, LR, HB, B), lambda step: (0, 0, 0, 0, 0))
            for piece in pieces
        ]
        + [anywhere] * 10,
        out_specs=[anywhere, anywhere, pl.BlockSpec((LR, B, B), lambda step: (0, 0, 0))],
        out_shape=[
            jax.ShapeDtypeStruct((PANEL, PANEL), bf16),
            jax.ShapeDtypeStruct((PANEL, PANEL), bf16),
            jax.ShapeDtypeStruct((LR, B, B), f32),
        ],
        scratch_shapes=[
            pltpu.VMEM((PANEL, PANEL), f32),
            pltpu.VMEM((PANEL, B), f32),
            pltpu.VMEM((COLS, 2, LR, HB, B), f32),
            pltpu.VMEM((PANEL, PANEL), bf16),
            pltpu.VMEM((PANEL, PANEL), bf16),
            pltpu.VMEM((PANEL, PANEL), bf16),
            pltpu.VMEM((PANEL, PANEL), bf16),
            pltpu.VMEM((PANEL, PANEL), f32),
            pltpu.VMEM((PANEL, PANEL), bf16),
            pltpu.VMEM((PANEL, PANEL), bf16),
            pltpu.VMEM((PANEL, PANEL), bf16),
            pltpu.VMEM((PANEL, PANEL), bf16),
            pltpu.SemaphoreType.DMA((COLS, 2)),
            pltpu.SemaphoreType.DMA((4, 2)),
        ],
        compiler_params=pltpu.CompilerParams(vmem_limit_bytes=VMEM),
        cost_estimate=CHEAP,
    )(*pieces, *pieces)


def trailing_update(table, upper, front, second, columns, high, low, panel):
    steps = LC // 2

    def body(tab, upper_ref, front_ref, second_ref, col_ref, high_ref, low_ref, panel_ref, out_ref,
             ch, cl, got, yh, yl, sem, left_sem):
        step = pl.program_id(0)

        def loads(r):
            rows = slice(r, r + 256)
            copies = []
            for m, (ref, held) in enumerate(((high_ref, yh), (low_ref, yl))):
                copies.append(
                    pltpu.make_async_copy(ref.at[rows], held.at[rows], left_sem.at[r // 256, m])
                )
            for child in range(2):
                for l in range(r // B, r // B + 2):
                    source = child * HALF + place_of(tab[child * NKEYS + l])
                    copies.append(
                        pltpu.make_async_copy(
                            second_ref.at[source], got.at[child, l], sem.at[child, l]
                        )
                    )
            return copies

        @pl.when(step == 0)
        def _():
            for r in range(0, PANEL, 256):
                for copy in loads(r):
                    copy.start()

        def products(first):
            for p in range(ROWS):
                top = (p % HALF) * B + (p // HALF) * HB
                for n in range(2):
                    hi, lo = split(col_ref[p, n])
                    ch[top : top + HB, n * B : (n + 1) * B] = hi
                    cl[top : top + HB, n * B : (n + 1) * B] = lo
            for r in range(0, PANEL, 256):
                if first:
                    for copy in loads(r):
                        copy.wait()
                value = block_dot(yh[r : r + 256, :], ch[...])
                value += block_dot(yh[r : r + 256, :], cl[...])
                value += block_dot(yl[r : r + 256, :], ch[...])
                for l in range(r // B, r // B + 2):
                    for n in range(2):
                        s = l * B - r
                        cols = slice(n * B, (n + 1) * B)
                        out_ref[l, n, :HB] = upper_ref[l, n] - value[s : s + HB, cols]
                        total = front_ref[l, n, 0]
                        for child in range(2):
                            base = child * NKEYS
                            code = tab[base + LR + 1 + 2 * step + n]
                            gain = gain_of(code) * gain_of(tab[base + l])
                            total = total + got[child, l, place_of(code)] * gain
                        out_ref[l, n, HB:] = total - value[s + HB : s + B, cols]

        @pl.when(step == 0)
        def _():
            products(True)
            for l in range(LR):
                out_ref[l, 0] = panel_ref[l]

        @pl.when(step > 0)
        def _():
            products(False)

    return pl.pallas_call(
        body,
        grid_spec=pltpu.PrefetchScalarGridSpec(
            num_scalar_prefetch=1,
            grid=(steps,),
            in_specs=[
                pl.BlockSpec((LR, 2, HB, B), lambda step, tab: (0, step, 0, 0)),
                pl.BlockSpec((LR, 2, 1, HB, B), lambda step, tab: (0, step, 1, 0, 0)),
                pl.BlockSpec(memory_space=pl.ANY),
                pl.BlockSpec((ROWS, 2, HB, B), lambda step, tab: (0, step, 0, 0)),
                pl.BlockSpec(memory_space=pl.ANY),
                pl.BlockSpec(memory_space=pl.ANY),
                pl.BlockSpec((LR, B, B), lambda step, tab: (0, 0, 0)),
            ],
            out_specs=pl.BlockSpec((LR, 2, B, B), lambda step, tab: (0, step, 0, 0)),
            scratch_shapes=[
                pltpu.VMEM((PANEL, 256), bf16),
                pltpu.VMEM((PANEL, 256), bf16),
                pltpu.VMEM((2, LR, COLS, HB, B), f32),
                pltpu.VMEM((PANEL, PANEL), bf16),
                pltpu.VMEM((PANEL, PANEL), bf16),
                pltpu.SemaphoreType.DMA((2, LR)),
                pltpu.SemaphoreType.DMA((4, 2)),
            ],
        ),
        out_shape=jax.ShapeDtypeStruct((LR, LC, B, B), f32),
        compiler_params=pltpu.CompilerParams(vmem_limit_bytes=VMEM),
        cost_estimate=CHEAP,
    )(table, upper, front, second, columns, high, low, panel)


def along_x(distance):
    return [(4 * ((x + distance) % 4) + z, 4 * x + z) for x in range(4) for z in range(4)]


def along_z(distance):
    return [(4 * x + (z + distance) % 4, 4 * x + z) for x in range(4) for z in range(4)]


def along_y(distance):
    return [(2 * ((y + distance) % 4) + k, 2 * y + k) for y in range(4) for k in range(2)]


OTHER_CORE = [(q, q ^ 1) for q in range(COLS)]


def transposed(same):
    pairs = []
    for p in range(ROWS):
        for q in range(COLS):
            side = p // HALF if same else 1 - p // HALF
            pairs.append((p * COLS + q, (q + HALF * side) * COLS + (p % HALF ^ q)))
    return pairs


def shards(parent_front, child_updates, child_mask, child_map):
    p = lax.axis_index("row")
    q = lax.axis_index("col")
    both = ("row", "col")
    front = parent_front.reshape(LR, LC, 2, HB, B)
    child = child_updates.reshape(CB, CB, 2, HB, B)

    own_map = child_map[p // HALF].reshape(CB, CB)
    row_parent = own_map[:, p % HALF]
    col_parent = own_map[:, q]
    index = jnp.arange(CB)
    column = jnp.sum((col_parent[None] % COLS == index[:, None]) * index[None], axis=1)
    source_table = jnp.concatenate([row_parent, column, child_mask.reshape(-1)]).astype(jnp.int32)

    keys = jnp.concatenate(
        [jnp.arange(LR) * ROWS + p, (p % HALF)[None], jnp.arange(LC) * COLS + q]
    )
    hits = child_map[:, None, :] == keys[None, :, None]
    codes = jnp.sum(hits * (jnp.arange(CB * CB) % CB + 1)[None, None], axis=2)
    target_table = jnp.concatenate([codes.reshape(-1), p[None]]).astype(jnp.int32)

    top_other = lax.ppermute(front[0, :, 1], "row", [(i, i + HALF) for i in range(HALF)])

    first = pack_slots(child, source_table, False)
    first = lax.all_to_all(
        first.reshape(ROWS * COLS, HB, B), both, 0, 0, tiled=True
    ).reshape(ROWS, COLS, HB, B)
    second = pack_slots(child, source_table, True)

    first, second = lax.optimization_barrier((first, second))
    target_table, top_other = lax.optimization_barrier((target_table, top_other))
    top, even, odd, lead = leading_row(front, top_other, first, target_table)

    turned = [
        lax.ppermute(even, both, transposed(True)),
        lax.ppermute(odd, both, transposed(False)),
    ]
    near = [lead] + [lax.ppermute(lead, "row", along_z(d)) for d in range(1, 4)]
    stacked = jnp.stack(near)
    near = [stacked] + [lax.ppermute(stacked, "row", along_x(d)) for d in range(1, 4)]
    packed = jnp.stack(
        [jnp.concatenate(near[:2]), turned[0], jnp.concatenate(near[2:]), turned[1]]
    ).reshape(2, 2, LR, HB, B)
    top, packed = lax.optimization_barrier((top, packed))

    columns = lax.all_gather(top, "row", axis=0)

    ahead = lax.ppermute(packed, "col", along_y(1))
    back = lax.ppermute(packed, "col", along_y(3))
    upper = extend_add(front, first, target_table, 0)
    upper, ahead, back = lax.optimization_barrier((upper, ahead, back))
    far = [
        lax.ppermute(ahead[:1], "col", along_y(1)),
        lax.ppermute(back[1:], "col", along_y(3)),
    ]
    second, far[0], far[1] = lax.optimization_barrier((second, far[0], far[1]))
    near = [packed, ahead, back] + far
    near = near + [lax.ppermute(piece, "col", OTHER_CORE) for piece in near]

    second = lax.all_to_all(
        second.reshape(ROWS * COLS, HB, B), both, 0, 0, tiled=True
    ).reshape(ROWS, COLS, HB, B)

    high, low, panel = factor_and_solve(near)
    high, columns = lax.optimization_barrier((high, columns))
    return trailing_update(target_table, upper, front, second, columns, high, low, panel)


def solution(mesh):
    in_specs = (P("row", "col", None, None), P("row", "col", None, None), P("row", "col"), P())
    out_specs = P("row", "col", None, None)
    return jax.shard_map(shards, mesh=mesh, in_specs=in_specs, out_specs=out_specs, check_vma=False)
```

```python
import jax
import jax.numpy as jnp
from jax import lax
from jax.experimental import pallas as pl
from jax.experimental.pallas import tpu as pltpu
from jax.sharding import PartitionSpec as P

B = 128
HB = 64
ROWS = 16
COLS = 8
HALF = 8
LR = 8
LC = 16
CB = 8
PANEL = 1024
f32 = jnp.float32
bf16 = jnp.bfloat16
exact = lax.Precision.HIGHEST
MIB = 2**20
VMEM = 62 * MIB
CHEAP = pl.CostEstimate(flops=2**10, bytes_accessed=2**10, transcendentals=0)


def block_dot(left, right, contract_left=1):
    dims = (((contract_left,), (0,)), ((), ()))
    return lax.dot_general(left, right, dims, preferred_element_type=f32)


def exact_dot(left, right, contract_left=1):
    dims = (((contract_left,), (0,)), ((), ()))
    return lax.dot_general(left, right, dims, precision=exact, preferred_element_type=f32)


def split(value):
    high = value.astype(bf16)
    return high, (value - high.astype(f32)).astype(bf16)


def pack_slots(child, table, second):
    def body(tab, child_ref, out_ref, held, packed, zero, in_sem, out_sem):
        halves = (1,) if second else (0, 1)
        size = len(halves)

        def fetch(i, n):
            return pltpu.make_async_copy(
                child_ref.at[i, :, halves[n]], held.at[i, n], in_sem.at[i, n]
            )

        def pack(i, n):
            fetch(i, n).wait()
            for place in range(COLS):
                source = tab[CB + place]
                gain = tab[2 * CB + i * CB + source].astype(f32)
                packed[i, n, place] = held[i, n, source] * gain

        for i in range(CB):
            fetch(i, 0).start()
        if not second:
            for i in range(CB):

                @pl.when(tab[i] < HALF)
                def _():
                    fetch(i, 1).start()

        zero[...] = jnp.zeros_like(zero)
        for i in range(CB):
            parent = tab[i]
            mine = parent % ROWS
            other = (mine + HALF) % ROWS
            pack(i, 0)
            pltpu.make_async_copy(packed.at[i, 0], out_ref.at[mine], out_sem.at[i, 0]).start()
            if second:
                pltpu.make_async_copy(zero, out_ref.at[other], out_sem.at[i, 1]).start()
            else:

                @pl.when(parent < HALF)
                def _():
                    pack(i, 1)
                    pltpu.make_async_copy(
                        packed.at[i, 1], out_ref.at[other], out_sem.at[i, 1]
                    ).start()

                @pl.when(parent >= HALF)
                def _():
                    pltpu.make_async_copy(zero, out_ref.at[other], out_sem.at[i, 1]).start()

        for i in range(CB):
            for n in range(2):
                pltpu.make_async_copy(zero, out_ref.at[0], out_sem.at[i, n]).wait()

    size = 1 if second else 2
    return pl.pallas_call(
        body,
        in_specs=[
            pl.BlockSpec(memory_space=pltpu.SMEM),
            pl.BlockSpec(memory_space=pl.ANY),
        ],
        out_specs=pl.BlockSpec(memory_space=pl.ANY),
        out_shape=jax.ShapeDtypeStruct((ROWS, COLS, HB, B), f32),
        scratch_shapes=[
            pltpu.VMEM((CB, size, CB, HB, B), f32),
            pltpu.VMEM((CB, size, COLS, HB, B), f32),
            pltpu.VMEM((COLS, HB, B), f32),
            pltpu.SemaphoreType.DMA((CB, size)),
            pltpu.SemaphoreType.DMA((CB, 2)),
        ],
        compiler_params=pltpu.CompilerParams(vmem_limit_bytes=VMEM),
        cost_estimate=CHEAP,
    )(table, child)


def gain_of(code):
    return (code > 0).astype(f32)


def place_of(code):
    return jnp.maximum(code - 1, 0)


NKEYS = LR + 1 + LC


def leading_row(front, received, arrived, table):
    def body(tab, own_ref, recv_ref, first_ref, other_ref, top_ref, even_ref, odd_ref, lead_ref):
        upper = tab[2 * NKEYS] < HALF
        side = tab[2 * NKEYS] // HALF
        for m in range(LC):
            value = jnp.where(upper, own_ref[0, m, 0], recv_ref[m])
            for child, ref in ((0, first_ref), (1, other_ref)):
                base = child * NKEYS
                code = tab[base + LR + 1 + m]
                gain = gain_of(code) * gain_of(tab[base + LR])
                value = value + ref[0, place_of(code)] * gain
            top_ref[m] = value
        lead_ref[...] = top_ref[0]
        for l in range(LR):
            even_ref[l] = top_ref[2 * l + side]
            odd_ref[l] = top_ref[2 * l + 1 - side]

    def rows_of(child):
        return lambda step, tab: (child * HALF + place_of(tab[child * NKEYS + LR]), 0, 0, 0)

    return pl.pallas_call(
        body,
        grid_spec=pltpu.PrefetchScalarGridSpec(
            num_scalar_prefetch=1,
            grid=(1,),
            in_specs=[
                pl.BlockSpec((1, LC, 1, HB, B), lambda step, tab: (0, 0, 0, 0, 0)),
                pl.BlockSpec((LC, HB, B), lambda step, tab: (0, 0, 0)),
                pl.BlockSpec((1, COLS, HB, B), rows_of(0)),
                pl.BlockSpec((1, COLS, HB, B), rows_of(1)),
            ],
            out_specs=[
                pl.BlockSpec((LC, HB, B), lambda step, tab: (0, 0, 0)),
                pl.BlockSpec((LR, HB, B), lambda step, tab: (0, 0, 0)),
                pl.BlockSpec((LR, HB, B), lambda step, tab: (0, 0, 0)),
                pl.BlockSpec((HB, B), lambda step, tab: (0, 0)),
            ],
        ),
        out_shape=[
            jax.ShapeDtypeStruct((LC, HB, B), f32),
            jax.ShapeDtypeStruct((LR, HB, B), f32),
            jax.ShapeDtypeStruct((LR, HB, B), f32),
            jax.ShapeDtypeStruct((HB, B), f32),
        ],
        compiler_params=pltpu.CompilerParams(vmem_limit_bytes=VMEM),
        cost_estimate=CHEAP,
    )(table, front, received, arrived, arrived)


def extend_add(front, arrived, table, half):
    def body(tab, parent_ref, first_ref, other_ref, out_ref):
        step = pl.program_id(0)
        for m in range(LC):
            value = parent_ref[0, m, 0]
            for child, ref in ((0, first_ref), (1, other_ref)):
                base = child * NKEYS
                code = tab[base + LR + 1 + m]
                gain = gain_of(code) * gain_of(tab[base + step])
                value = value + ref[0, place_of(code)] * gain
            out_ref[0, m] = value

    def rows_of(child):
        return lambda step, tab: (child * HALF + place_of(tab[child * NKEYS + step]), 0, 0, 0)

    return pl.pallas_call(
        body,
        grid_spec=pltpu.PrefetchScalarGridSpec(
            num_scalar_prefetch=1,
            grid=(LR,),
            in_specs=[
                pl.BlockSpec((1, LC, 1, HB, B), lambda step, tab: (step, 0, half, 0, 0)),
                pl.BlockSpec((1, COLS, HB, B), rows_of(0)),
                pl.BlockSpec((1, COLS, HB, B), rows_of(1)),
            ],
            out_specs=pl.BlockSpec((1, LC, HB, B), lambda step, tab: (step, 0, 0, 0)),
        ),
        out_shape=jax.ShapeDtypeStruct((LR, LC, HB, B), f32),
        compiler_params=pltpu.CompilerParams(vmem_limit_bytes=VMEM),
        cost_estimate=CHEAP,
    )(table, front, arrived, arrived)


def factor_block(block):
    lane = lax.broadcasted_iota(jnp.int32, (8, B), 1)
    sub = lax.broadcasted_iota(jnp.int32, (8, B), 0)

    def lanes(tile, j):
        return jnp.broadcast_to(tile[:, j : j + 1], (8, B))

    def subs(tile, k):
        return jnp.broadcast_to(tile[k : k + 1, :], (8, B))

    tiles = [block[8 * r : 8 * r + 8, :] for r in range(B // 8)]
    for group in range(B // 8):
        low = 8 * group
        own = [lanes(tiles[group], low + k) for k in range(8)]
        work = tiles[group]
        inside = jnp.logical_and(lane >= low, lane < low + 8)
        upper = []
        for k in range(0, 8, 2):
            n = k + 1
            a, b, c = subs(own[k], k), subs(own[n], k), subs(own[n], n)
            det = 1.0 / (a * c - b * b)
            at_k, at_n = lane == low + k, lane == low + n
            on_k, on_n = sub == k, sub == n
            on = jnp.logical_or(on_k, on_n)
            row_k, row_n = subs(work, k), subs(work, n)
            upper.append(row_k)
            ratio = b * (1.0 / a)
            upper.append(jnp.where(at_k, 0.0, row_n) - ratio * jnp.where(at_k, 1.0, row_k))
            row_k = jnp.where(at_k, 1.0, jnp.where(at_n, 0.0, row_k))
            row_n = jnp.where(at_n, 1.0, jnp.where(at_k, 0.0, row_n))
            new_k = c * row_k - b * row_n
            new_n = a * row_n - b * row_k
            coef_k = jnp.where(on_k, -1.0, jnp.where(on_n, 0.0, own[k]))
            coef_n = jnp.where(on_n, -1.0, jnp.where(on_k, 0.0, own[n]))
            clear = jnp.logical_or(jnp.logical_or(at_k, at_n), on)
            work = jnp.where(clear, 0.0, work) - det * (coef_k * new_k + coef_n * new_n)
            for m in range(k + 2, 8):
                x, y = subs(own[m], k), subs(own[m], n)
                step = coef_k * (c * x - b * y) + coef_n * (a * y - b * x)
                own[m] = jnp.where(on, 0.0, own[m]) - det * step
        solved = [subs(work, k) for k in range(8)]
        rows = upper[0]
        for k in range(1, 8):
            rows = jnp.where(sub == k, upper[k], rows)
        tiles[group] = rows
        for r in range(group + 1, B // 8):
            value = jnp.where(inside, 0.0, tiles[r])
            for k in range(8):
                value = value - lanes(tiles[r], low + k) * solved[k]
            tiles[r] = value
    return jnp.concatenate(tiles, axis=0)


def factor_and_solve(pieces):
    def origin(at, n):
        dk, dy = n // 5, (0, 1, 3, 2, 2)[n % 5]
        return ((at[2] + dy) % 4) * 2 + (at[3] + dk) % 2

    def body(*refs):
        lead_refs, rows_refs, refs = refs[:10], refs[10:20], refs[20:]
        high_ref, low_ref, out_ref, w, diag, rows, gh, gl, wh, wl, below, bh, bl = refs[:13]
        yh, yl, sem, out_sem = refs[13:]
        p = lax.axis_index("row")
        q = lax.axis_index("col")
        at = (p // 4, p % 4, q // 2, q % 2)
        side = p // HALF
        copies = []
        for n, ref in enumerate(rows_refs):
            e = origin(at, n) ^ (p % HALF)
            for half in range(ref.shape[0]):
                order = 1 if n % 5 == 4 else half
                copies.append(
                    pltpu.make_async_copy(ref.at[half, 1], rows.at[e, order], sem.at[e, order])
                )
        for copy in copies:
            copy.start()
        for n, ref in enumerate(lead_refs):
            e = origin(at, n)
            for half in range(ref.shape[0]):
                for place in range(LR):
                    dx = half * 2 + place // 4 + (2 if n % 5 == 4 else 0)
                    x, z = (at[0] + dx) % 4, (at[1] + place) % 4
                    g = (x % 2) * 4 + z
                    top = pl.multiple_of(g * B + (x // 2) * HB, HB)
                    w[pl.ds(top, HB), pl.ds(pl.multiple_of(e * B, B), B)] = ref[half, 0, place]
        row = lax.broadcasted_iota(jnp.int32, (B, B), 0)
        col = lax.broadcasted_iota(jnp.int32, (B, B), 1)
        def finish(f, o):
            pivots = jnp.sum(jnp.where(row == col, f, 0.0), axis=1, keepdims=True)
            scale = 1.0 / jnp.sqrt(pivots)
            diag[pl.ds(o, B), :] = jnp.where(row <= col, f, 0.0) * scale
            return jnp.where(row > col, f, (row == col).astype(f32)) * scale

        def step(j, carry):
            o = pl.multiple_of(j * 256, 256)
            n = pl.multiple_of(o + B, B)
            inverse = finish(factor_block(w[pl.ds(o, B), pl.ds(o, B)]), o)
            above = exact_dot(inverse, w[pl.ds(o, B), pl.ds(n, B)])
            f = factor_block(w[pl.ds(n, B), pl.ds(n, B)] - exact_dot(above, above, 0))
            w[pl.ds(o, B), :] = exact_dot(inverse, w[pl.ds(o, B), :])
            w[pl.ds(o, B), pl.ds(o, B)] = inverse
            w[pl.ds(n, B), pl.ds(o, B)] = jnp.zeros((B, B), f32)
            w[pl.ds(n, B), :] -= exact_dot(w[pl.ds(o, B), pl.ds(n, B)], w[pl.ds(o, B), :], 0)
            inverse = finish(f, n)
            w[pl.ds(n, B), :] = exact_dot(inverse, w[pl.ds(n, B), :])
            w[pl.ds(n, B), pl.ds(n, B)] = inverse

            for done in range(256, PANEL, 256):

                @pl.when(j == done // 256 - 1)
                def _():
                    above = (slice(done - 256, done - B), slice(done - B, done))
                    kept = w[above]
                    w[above] = jnp.zeros((B, B), f32)
                    w[done:, done - 256 : done] = jnp.zeros((PANEL - done, 256), f32)
                    for i in range(done, PANEL, 256):
                        left = w[done - 256 : done, i : i + 256]
                        for part in (slice(0, done), slice(i, PANEL)):
                            w[i : i + 256, part] -= exact_dot(left, w[done - 256 : done, part], 0)
                    w[above] = kept

            return carry

        lax.fori_loop(0, PANEL // 256, step, 0)

        for copy in copies:
            copy.wait()
        for e in range(COLS):
            for order in range(2):
                half = side if order == 0 else 1 - side
                top = pl.multiple_of(e * B + half * HB, HB)
                for l in range(LR):
                    high, low = split(rows[e, order, l])
                    gh[pl.ds(top, HB), l * B : (l + 1) * B] = high
                    gl[pl.ds(top, HB), l * B : (l + 1) * B] = low
        for r in range(0, PANEL, 256):
            shape = (256, r + 256)
            under = (
                lax.broadcasted_iota(jnp.int32, shape, 0) + r
                >= lax.broadcasted_iota(jnp.int32, shape, 1)
            )
            high, low = split(jnp.where(under, w[r : r + 256, : r + 256], 0.0))
            wh[r : r + 256, : r + 256] = high
            wl[r : r + 256, : r + 256] = low
            value = block_dot(high, gh[: r + 256, :])
            value += block_dot(high, gl[: r + 256, :])
            value += block_dot(low, gh[: r + 256, :])
            for l in range(LR):
                for n in range(0, 256, B):
                    tile = value[n : n + B, l * B : (l + 1) * B].T
                    high, low = split(tile)
                    place = (slice(l * B, (l + 1) * B), slice(r + n, r + n + B))
                    below[place] = tile
                    bh[place] = high
                    bl[place] = low
        mine = pl.ds(pl.multiple_of(q * B, B), B)
        for l in range(LR):
            out_ref[l] = below[l * B : (l + 1) * B, mine]

        @pl.when(p < HALF)
        def _():
            over = w[mine, pl.ds(pl.multiple_of((p % HALF) * B, B), B)]
            top = jnp.where(p > q, over, jnp.where(p == q, diag[mine, :], 0.0))
            out_ref[0] = top.T

        @pl.when(p < HALF)
        def _():
            bh[:B, :] = jnp.zeros((B, PANEL), bf16)
            bl[:B, :] = jnp.zeros((B, PANEL), bf16)

        sends = []
        for n, r in enumerate(range(0, PANEL, 256)):
            cols = slice(r, r + 256)
            value = block_dot(bh[:, r:], wh[r:, cols])
            value += block_dot(bl[:, r:], wh[r:, cols])
            value += block_dot(bh[:, r:], wl[r:, cols])
            yh[:, cols], yl[:, cols] = split(value)
            for m, (held, ref) in enumerate(((yh, high_ref), (yl, low_ref))):
                sends.append(
                    pltpu.make_async_copy(held.at[:, cols], ref.at[:, cols], out_sem.at[n, m])
                )
                sends[-1].start()
        for send in sends:
            send.wait()

    anywhere = pl.BlockSpec(memory_space=pl.ANY)
    return pl.pallas_call(
        body,
        grid=(1,),
        in_specs=[
            pl.BlockSpec((piece.shape[0], 1, LR, HB, B), lambda step: (0, 0, 0, 0, 0))
            for piece in pieces
        ]
        + [anywhere] * 10,
        out_specs=[anywhere, anywhere, pl.BlockSpec((LR, B, B), lambda step: (0, 0, 0))],
        out_shape=[
            jax.ShapeDtypeStruct((PANEL, PANEL), bf16),
            jax.ShapeDtypeStruct((PANEL, PANEL), bf16),
            jax.ShapeDtypeStruct((LR, B, B), f32),
        ],
        scratch_shapes=[
            pltpu.VMEM((PANEL, PANEL), f32),
            pltpu.VMEM((PANEL, B), f32),
            pltpu.VMEM((COLS, 2, LR, HB, B), f32),
            pltpu.VMEM((PANEL, PANEL), bf16),
            pltpu.VMEM((PANEL, PANEL), bf16),
            pltpu.VMEM((PANEL, PANEL), bf16),
            pltpu.VMEM((PANEL, PANEL), bf16),
            pltpu.VMEM((PANEL, PANEL), f32),
            pltpu.VMEM((PANEL, PANEL), bf16),
            pltpu.VMEM((PANEL, PANEL), bf16),
            pltpu.VMEM((PANEL, PANEL), bf16),
            pltpu.VMEM((PANEL, PANEL), bf16),
            pltpu.SemaphoreType.DMA((COLS, 2)),
            pltpu.SemaphoreType.DMA((4, 2)),
        ],
        compiler_params=pltpu.CompilerParams(vmem_limit_bytes=VMEM),
        cost_estimate=CHEAP,
    )(*pieces, *pieces)


def trailing_update(table, upper, front, second, columns, high, low, panel):
    steps = LC // 2

    def body(tab, upper_ref, front_ref, second_ref, col_ref, high_ref, low_ref, panel_ref, out_ref,
             ch, cl, got, yh, yl, sem, left_sem):
        step = pl.program_id(0)

        def loads(r):
            rows = slice(r, r + 256)
            copies = []
            for m, (ref, held) in enumerate(((high_ref, yh), (low_ref, yl))):
                copies.append(
                    pltpu.make_async_copy(ref.at[rows], held.at[rows], left_sem.at[r // 256, m])
                )
            for child in range(2):
                for l in range(r // B, r // B + 2):
                    source = child * HALF + place_of(tab[child * NKEYS + l])
                    copies.append(
                        pltpu.make_async_copy(
                            second_ref.at[source], got.at[child, l], sem.at[child, l]
                        )
                    )
            return copies

        @pl.when(step == 0)
        def _():
            for r in range(0, PANEL, 256):
                for copy in loads(r):
                    copy.start()

        def products(first):
            for p in range(ROWS):
                top = (p % HALF) * B + (p // HALF) * HB
                for n in range(2):
                    hi, lo = split(col_ref[p, n])
                    ch[top : top + HB, n * B : (n + 1) * B] = hi
                    cl[top : top + HB, n * B : (n + 1) * B] = lo
            for r in range(0, PANEL, 256):
                if first:
                    for copy in loads(r):
                        copy.wait()
                value = block_dot(yh[r : r + 256, :], ch[...])
                value += block_dot(yh[r : r + 256, :], cl[...])
                value += block_dot(yl[r : r + 256, :], ch[...])
                for l in range(r // B, r // B + 2):
                    for n in range(2):
                        s = l * B - r
                        cols = slice(n * B, (n + 1) * B)
                        out_ref[l, n, :HB] = upper_ref[l, n] - value[s : s + HB, cols]
                        total = front_ref[l, n, 0]
                        for child in range(2):
                            base = child * NKEYS
                            code = tab[base + LR + 1 + 2 * step + n]
                            gain = gain_of(code) * gain_of(tab[base + l])
                            total = total + got[child, l, place_of(code)] * gain
                        out_ref[l, n, HB:] = total - value[s + HB : s + B, cols]

        @pl.when(step == 0)
        def _():
            products(True)
            for l in range(LR):
                out_ref[l, 0] = panel_ref[l]

        @pl.when(step > 0)
        def _():
            products(False)

    return pl.pallas_call(
        body,
        grid_spec=pltpu.PrefetchScalarGridSpec(
            num_scalar_prefetch=1,
            grid=(steps,),
            in_specs=[
                pl.BlockSpec((LR, 2, HB, B), lambda step, tab: (0, step, 0, 0)),
                pl.BlockSpec((LR, 2, 1, HB, B), lambda step, tab: (0, step, 1, 0, 0)),
                pl.BlockSpec(memory_space=pl.ANY),
                pl.BlockSpec((ROWS, 2, HB, B), lambda step, tab: (0, step, 0, 0)),
                pl.BlockSpec(memory_space=pl.ANY),
                pl.BlockSpec(memory_space=pl.ANY),
                pl.BlockSpec((LR, B, B), lambda step, tab: (0, 0, 0)),
            ],
            out_specs=pl.BlockSpec((LR, 2, B, B), lambda step, tab: (0, step, 0, 0)),
            scratch_shapes=[
                pltpu.VMEM((PANEL, 256), bf16),
                pltpu.VMEM((PANEL, 256), bf16),
                pltpu.VMEM((2, LR, COLS, HB, B), f32),
                pltpu.VMEM((PANEL, PANEL), bf16),
                pltpu.VMEM((PANEL, PANEL), bf16),
                pltpu.SemaphoreType.DMA((2, LR)),
                pltpu.SemaphoreType.DMA((4, 2)),
            ],
        ),
        out_shape=jax.ShapeDtypeStruct((LR, LC, B, B), f32),
        compiler_params=pltpu.CompilerParams(vmem_limit_bytes=VMEM),
        cost_estimate=CHEAP,
    )(table, upper, front, second, columns, high, low, panel)


def along_x(distance):
    return [(4 * ((x + distance) % 4) + z, 4 * x + z) for x in range(4) for z in range(4)]


def along_z(distance):
    return [(4 * x + (z + distance) % 4, 4 * x + z) for x in range(4) for z in range(4)]


def along_y(distance):
    return [(2 * ((y + distance) % 4) + k, 2 * y + k) for y in range(4) for k in range(2)]


OTHER_CORE = [(q, q ^ 1) for q in range(COLS)]


def transposed(same):
    pairs = []
    for p in range(ROWS):
        for q in range(COLS):
            side = p // HALF if same else 1 - p // HALF
            pairs.append((p * COLS + q, (q + HALF * side) * COLS + (p % HALF ^ q)))
    return pairs


def shards(parent_front, child_updates, child_mask, child_map):
    p = lax.axis_index("row")
    q = lax.axis_index("col")
    both = ("row", "col")
    front = parent_front.reshape(LR, LC, 2, HB, B)
    child = child_updates.reshape(CB, CB, 2, HB, B)

    own_map = child_map[p // HALF].reshape(CB, CB)
    row_parent = own_map[:, p % HALF]
    col_parent = own_map[:, q]
    index = jnp.arange(CB)
    column = jnp.sum((col_parent[None] % COLS == index[:, None]) * index[None], axis=1)
    source_table = jnp.concatenate([row_parent, column, child_mask.reshape(-1)]).astype(jnp.int32)

    keys = jnp.concatenate(
        [jnp.arange(LR) * ROWS + p, (p % HALF)[None], jnp.arange(LC) * COLS + q]
    )
    hits = child_map[:, None, :] == keys[None, :, None]
    codes = jnp.sum(hits * (jnp.arange(CB * CB) % CB + 1)[None, None], axis=2)
    target_table = jnp.concatenate([codes.reshape(-1), p[None]]).astype(jnp.int32)

    top_other = lax.ppermute(front[0, :, 1], "row", [(i, i + HALF) for i in range(HALF)])

    first = pack_slots(child, source_table, False)
    first = lax.all_to_all(
        first.reshape(ROWS * COLS, HB, B), both, 0, 0, tiled=True
    ).reshape(ROWS, COLS, HB, B)
    second = pack_slots(child, source_table, True)

    first, second = lax.optimization_barrier((first, second))
    target_table, top_other = lax.optimization_barrier((target_table, top_other))
    top, even, odd, lead = leading_row(front, top_other, first, target_table)

    turned = [
        lax.ppermute(even, both, transposed(True)),
        lax.ppermute(odd, both, transposed(False)),
    ]
    near = [lead] + [lax.ppermute(lead, "row", along_z(d)) for d in range(1, 4)]
    stacked = jnp.stack(near)
    near = [stacked] + [lax.ppermute(stacked, "row", along_x(d)) for d in range(1, 4)]
    packed = jnp.stack(
        [jnp.concatenate(near[:2]), turned[0], jnp.concatenate(near[2:]), turned[1]]
    ).reshape(2, 2, LR, HB, B)
    top, packed = lax.optimization_barrier((top, packed))

    columns = lax.all_gather(top, "row", axis=0)

    ahead = lax.ppermute(packed, "col", along_y(1))
    back = lax.ppermute(packed, "col", along_y(3))
    upper = extend_add(front, first, target_table, 0)
    upper, ahead, back = lax.optimization_barrier((upper, ahead, back))
    far = [
        lax.ppermute(ahead[:1], "col", along_y(1)),
        lax.ppermute(back[1:], "col", along_y(3)),
    ]
    second, far[0], far[1] = lax.optimization_barrier((second, far[0], far[1]))
    near = [packed, ahead, back] + far
    near = near + [lax.ppermute(piece, "col", OTHER_CORE) for piece in near]

    second = lax.all_to_all(
        second.reshape(ROWS * COLS, HB, B), both, 0, 0, tiled=True
    ).reshape(ROWS, COLS, HB, B)

    high, low, panel = factor_and_solve(near)
    high, columns = lax.optimization_barrier((high, columns))
    return trailing_update(target_table, upper, front, second, columns, high, low, panel)


def solution(mesh):
    in_specs = (P("row", "col", None, None), P("row", "col", None, None), P("row", "col"), P())
    out_specs = P("row", "col", None, None)
    return jax.shard_map(shards, mesh=mesh, in_specs=in_specs, out_specs=out_specs, check_vma=False)
```
